256 devices in a mesh: gx: 16 (over z, y_hi), gy: 16 (over y_lo, x, core).
Axes of the slice: x: 4, y: 4 (y_hi: 2, y_lo: 2; y = y_hi * 2 + y_lo), z: 8, core: 2. Of those that a mesh axis runs over, the one named last changes fastest.
Arguments:
- populations: float32 [19, 64, 128, 128], P(None, 'gx', 'gy'), may hold values from 0.02 to 0.1
- flags: int32 [64, 128, 128], P('gx', 'gy'), may hold values from 0 to 1, as said below
- block_tile: int32 [4096, 1], P(('gx', 'gy')), may hold values from 0 to 15; in each aligned block of 16 rows (0 to 15, 16 to 31, ...) at most 2 rows name the same one
- marker_cell: int32 [4096, 128], P(('gx', 'gy')), may hold values from 1 to 2941, as said below
- marker_frac: float32 [4096, 3, 128], P(('gx', 'gy')), may hold values from 0 to 1
- marker_live: int32 [4096, 128], P(('gx', 'gy')), may hold values 0 or 1
- marker_target: float32 [4096, 3, 128], P(('gx', 'gy')), may hold values from -0.3 to 0.3
- marker_force: float32 [4096, 3, 128], P(('gx', 'gy')), may hold values from -0.3 to 0.3
Outputs:
- populations_out: float32 [19, 64, 128, 128], P(None, 'gx', 'gy')
- marker_force_out: float32 [4096, 3, 128], P(('gx', 'gy'))
The draws below stay inside these ranges and needn't reach their ends.
Inputs may be any that keep to these rules, and one draw needn't show every extreme that they name: `flags`: every cell of the first and of the last layer along z is a wall. `block_tile`: A block's tile lies in its owner's gy column; among the 16 rows of one device at most 2 name the same tile. `marker_cell`: equal to (i * 8 + j) * 128 + k with i < 3, j < 7 and 1 <= k < 126, so a marker's box lies inside its tile.
All inputs are finite; a program needn't handle non-finite values. No bound on the sum of `marker_live` on one device may be relied on, other than what follows from the above.
Results may differ from the reference program's by a relative error of at most 0.0001.
Values sent between devices are 32-bit elements; how exact they have to be, the bound alone decides.
A program may use at most 64 MiB of HBM per device.

```python
import math
import jax
import jax.numpy as jnp
import numpy as np
from jax import lax

CX = 4
CY = 8
NZ = 128
STEPS = 2
MB = 16
MARK = 128
SLOT = 2
NX = 64
NY = 128
BLOCKS = 4096
N_GX = 16
N_GY = 16


def draw_flags(key, part):
    key = jax.random.fold_in(key, 11)
    rolled = jax.random.randint(key, (NX, NY, NZ), 0, 16)
    depth = lax.broadcasted_iota(jnp.int32, (NX, NY, NZ), 2)
    solid = (rolled == 0) | (depth == 0) | (depth == NZ - 1)
    return solid.astype(jnp.int32)


def draw_marker_cell(key, part):
    key = jax.random.fold_in(key, 23)
    key_east, key_north, key_upper = jax.random.split(key, 3)
    east_cell = jax.random.randint(key_east, (BLOCKS, MARK), 0, CX - 1)
    north_cell = jax.random.randint(key_north, (BLOCKS, MARK), 0, CY - 1)
    upper_cell = jax.random.randint(key_upper, (BLOCKS, MARK), 1, NZ - 2)
    cells = (east_cell * CY + north_cell) * NZ + upper_cell
    highest = ((CX - 2) * CY + CY - 2) * NZ + NZ - 3
    cells = cells.at[0, 0].set(1)
    cells = cells.at[0, 1].set(highest)
    return cells.astype(jnp.int32)


def plant(entries, own_key, least, largest):
    longest = entries.shape.index(max(entries.shape))
    spots = []
    for shift in (0, 1):
        where = [jax.random.randint(jax.random.fold_in(own_key, axis), (), 0, length) for axis, length in enumerate(entries.shape)]
        where[longest] = (where[longest] + shift) % entries.shape[longest]
        spots.append(tuple(where))
    return entries.at[spots[0]].set(least).at[spots[1]].set(largest)


def block_levels(stream_key, dims, cuts, low, largest):
    level, own = 1.0, jax.random.fold_in(stream_key, 6)
    for dim, blocks in cuts:
        steps = jnp.exp(jax.random.uniform(jax.random.fold_in(own, dim), (blocks,), jnp.float32, low / len(cuts), largest / len(cuts)))
        level = level * jnp.repeat(steps, dims[dim] // blocks).reshape([-1 if axis == dim else 1 for axis in range(len(dims))])
    return level


def shared_out(own_key, own, number, rows, count, top, limit, lean):
    sequence = jax.random.permutation(own_key, count)
    crowded, ordinary = portions_of(count, rows * top, limit, lean, True), portions_of(count, rows * top, limit, lean, False)
    places = jnp.arange(count)

    def named(tallies, turn):
        used = int((tallies > 0).sum())
        fixed = max(1, used // 4)
        moved = fixed + (places - fixed + turn * (used - fixed)) % max(1, count - fixed)
        return jnp.zeros((count,), jnp.int32).at[sequence[jnp.where(places < fixed, places, moved)]].set(jnp.asarray(tallies, jnp.int32))

    tallies = jnp.where(number % 4 == 0, named(crowded, number // 4), named(ordinary, number - number // 4 - 1))
    mixed = jax.random.permutation(jax.random.fold_in(own, 3), count)
    giver, receiver = mixed[0:count // 2 * 2:2], mixed[1:count // 2 * 2:2]
    room = jnp.minimum(tallies[giver] - 1, limit - tallies[receiver]) // 2
    room = jnp.where((giver == sequence[0]) | (receiver == sequence[0]) | (tallies[receiver] == 0), 0, jnp.maximum(room, 0))
    moved = jax.random.randint(jax.random.fold_in(own, 4), (count // 2,), 0, 1 << 20) % (room + 1)
    tallies = tallies.at[giver].add(-moved).at[receiver].add(moved)
    items = jnp.searchsorted(jnp.cumsum(tallies), jnp.arange(rows * top), side="right").astype(jnp.int32)
    grid = items.reshape(top, rows).T
    grid = grid[jax.random.permutation(jax.random.fold_in(own, 1), rows)]
    turn = jax.random.randint(jax.random.fold_in(own, 2), (rows, 1), 0, top)
    return jnp.take_along_axis(grid, (jnp.arange(top)[None, :] + turn) % top, axis=1)


def portions_of(amount, total, limit, skew, full):
    loads = [(1 << 20) // math.isqrt(standing ** skew) + 1 for standing in range(1, amount + 1)]
    largest = limit if full else min(limit, max(-(-total // amount), total * loads[0] // sum(loads)))
    least = 1 if total - largest >= amount - 1 else 0
    counts, spare = [largest] + [least] * (amount - 1), total - largest - least * (amount - 1)
    while spare > 0:
        movable = [i for i in range(1, amount) if counts[i] < largest] or [i for i in range(1, amount) if counts[i] < limit]
        whole, remaining = sum([loads[i] for i in movable]), spare
        for i in movable:
            addition = min(limit - counts[i], max(1, remaining * loads[i] // whole), spare)
            counts[i] = counts[i] + addition
            spare = spare - addition
    return np.array(counts)


def normal_values(own_key, dims, spread, limit, pieces=(), held_as=jnp.bfloat16):
    values = spread * jax.random.normal(own_key, dims, jnp.float32)
    if pieces:
        values = values * block_levels(own_key, dims, pieces, -0.22, 0.18)
    return jnp.clip(values, -limit, limit).astype(held_as)


def setup_inputs(seed: int = 0) -> dict:
    key_of = jax.random.split(jax.random.key(seed), 9)
    populations = jnp.clip(0.02 + 0.08 * jax.random.uniform(key_of[0], (19, NX, NY, NZ), jnp.float32) ** block_levels(key_of[0], (19, NX, NY, NZ), ((1, 16), (2, 16)), -0.2, 0.2), 0.02, 0.1)
    flags = draw_flags(jax.random.fold_in(key_of[8], 71), 0)
    block_tile_keys = jax.random.split(jax.random.fold_in(key_of[2], 1), BLOCKS // MB)
    block_tile_turns = jax.random.permutation(jax.random.fold_in(key_of[2], 3), BLOCKS // MB)
    block_tile = jax.vmap(lambda own, number: shared_out(jax.random.fold_in(key_of[2], 2), own, number, MB, N_GX, 1, SLOT, 2))(block_tile_keys, block_tile_turns).reshape((BLOCKS, 1))
    marker_cell = draw_marker_cell(jax.random.fold_in(key_of[8], 71), 0)
    marker_frac = jnp.clip(1.0 * jax.random.uniform(key_of[4], (BLOCKS, 3, MARK), jnp.float32) ** block_levels(key_of[4], (BLOCKS, 3, MARK), ((0, 256),), -0.2, 0.2), 0.0, 1.0)
    marker_live = plant((jax.random.randint(key_of[5], (BLOCKS, MARK), 0, 4) < 3).astype(jnp.int32), jax.random.fold_in(key_of[5], 1), 0, 1)
    marker_target = normal_values(key_of[6], (BLOCKS, 3, MARK), 0.05, 0.3, ((0, 256),), jnp.float32)
    marker_force = normal_values(key_of[7], (BLOCKS, 3, MARK), 0.05, 0.3, ((0, 256),), jnp.float32)
    return {"populations": populations, "flags": flags, "block_tile": block_tile, "marker_cell": marker_cell, "marker_frac": marker_frac, "marker_live": marker_live, "marker_target": marker_target, "marker_force": marker_force}


VELOCITIES = ((0, 0, 0), (1, 0, 0), (-1, 0, 0), (0, 1, 0), (0, -1, 0), (0, 0, 1), (0, 0, -1),
              (1, 1, 0), (-1, -1, 0), (1, -1, 0), (-1, 1, 0), (1, 0, 1), (-1, 0, -1), (1, 0, -1),
              (-1, 0, 1), (0, 1, 1), (0, -1, -1), (0, 1, -1), (0, -1, 1))
OPPOSITE = (0, 2, 1, 4, 3, 6, 5, 8, 7, 10, 9, 12, 11, 14, 13, 16, 15, 18, 17)
WEIGHTS = (1.0 / 3.0,) + (1.0 / 18.0,) * 6 + (1.0 / 36.0,) * 12
OMEGA = 1.25


def project(vector, direction):
    result = jnp.zeros_like(vector[0])
    for component in range(3):
        factor = VELOCITIES[direction][component]
        if factor != 0:
            result = result + factor * vector[component]
    return result


def moments(populations):
    density = jnp.sum(populations, axis=0)
    parts_list = []
    for component in range(3):
        result = jnp.zeros_like(density)
        for direction in range(19):
            factor = VELOCITIES[direction][component]
            if factor != 0:
                result = result + factor * populations[direction]
        parts_list.append(result / density)
    return density, jnp.stack(parts_list)


def collide(populations, density, velocity, forcing):
    shifted = velocity + forcing / (2.0 * density)
    squared = shifted[0] * shifted[0] + shifted[1] * shifted[1] + shifted[2] * shifted[2]
    power = shifted[0] * forcing[0] + shifted[1] * forcing[1] + shifted[2] * forcing[2]
    outputs = []
    for direction in range(19):
        speed_along = project(shifted, direction)
        force_along = project(forcing, direction)
        equilibrium = WEIGHTS[direction] * density * (1.0 + 3.0 * speed_along + 4.5 * speed_along * speed_along - 1.5 * squared)
        source = (1.0 - 0.5 * OMEGA) * WEIGHTS[direction] * (3.0 * (force_along - power) + 9.0 * speed_along * force_along)
        current = populations[direction]
        outputs.append(current - OMEGA * (current - equilibrium) + source)
    return jnp.stack(outputs)


def corner_weights(fractions, marker_live):
    alive = marker_live.astype(jnp.float32)
    factors = []
    for corner in range(8):
        product = alive
        for axis_number, bit_value in ((0, corner // 4), (1, corner // 2 % 2), (2, corner % 2)):
            if bit_value:
                product = product * fractions[:, axis_number]
            else:
                product = product * (1.0 - fractions[:, axis_number])
        factors.append(product)
    return jnp.stack(factors, axis=1)


def reference(populations, flags, block_tile, marker_cell, marker_frac, marker_live, marker_target, marker_force):
    weights = corner_weights(marker_frac, marker_live)
    live_float = marker_live.astype(jnp.float32)[:, None, :]
    owner = jnp.arange(BLOCKS, dtype=jnp.int32) // MB
    column = owner % N_GY
    tile = block_tile[:, 0]
    local_x = marker_cell // (CY * NZ)
    local_y = (marker_cell // NZ) % CY
    local_z = marker_cell % NZ
    base = ((tile[:, None] * CX + local_x) * NY + column[:, None] * CY + local_y) * NZ + local_z
    offsets = jnp.array([(corner // 4) * NY * NZ + (corner // 2 % 2) * NZ + corner % 2 for corner in range(8)], dtype=jnp.int32)
    index = base[:, None, :] + offsets[None, :, None]
    flat_index = index.reshape(-1)
    force = marker_force
    state = populations
    for step_number in range(STEPS):
        density, velocity = moments(state)
        flat_velocity = velocity.reshape(3, -1)
        sampled = jnp.sum(weights[None] * flat_velocity[:, index], axis=2).transpose(1, 0, 2)
        force = force + live_float * (marker_target - sampled)
        contrib = (weights[:, None] * force[:, :, None]).transpose(1, 0, 2, 3).reshape(3, -1)
        field = jnp.zeros((3, NX * NY * NZ), jnp.float32).at[:, flat_index].add(contrib).reshape(3, NX, NY, NZ)
        post = collide(state, density, velocity, field)
        outputs = []
        for direction in range(19):
            east_step, north_step, upward_step = VELOCITIES[direction]
            pulled = jnp.roll(post[direction], (east_step, north_step, upward_step), axis=(0, 1, 2))
            solid = jnp.roll(flags, (east_step, north_step, upward_step), axis=(0, 1, 2))
            outputs.append(jnp.where(solid == 1, post[OPPOSITE[direction]], pulled))
        state = jnp.stack(outputs)
    return state, force
```

```python
import functools

import jax
import jax.numpy as jnp
from jax import lax
from jax.experimental import pallas as pl
from jax.experimental.pallas import tpu as pltpu
from jax.sharding import PartitionSpec as P

STEPS = 2
SLOT = 2
MESH = pl.DeviceIdType.MESH

VELOCITIES = (
    (0, 0, 0),
    (1, 0, 0),
    (-1, 0, 0),
    (0, 1, 0),
    (0, -1, 0),
    (0, 0, 1),
    (0, 0, -1),
    (1, 1, 0),
    (-1, -1, 0),
    (1, -1, 0),
    (-1, 1, 0),
    (1, 0, 1),
    (-1, 0, -1),
    (1, 0, -1),
    (-1, 0, 1),
    (0, 1, 1),
    (0, -1, -1),
    (0, 1, -1),
    (0, -1, 1),
)
OPPOSITE = (0, 2, 1, 4, 3, 6, 5, 8, 7, 10, 9, 12, 11, 14, 13, 16, 15, 18, 17)
WEIGHTS = (1.0 / 3.0,) + (1.0 / 18.0,) * 6 + (1.0 / 36.0,) * 12
OMEGA = 1.25

EAST = tuple(d for d in range(19) if VELOCITIES[d][0] == 1)
WEST = tuple(d for d in range(19) if VELOCITIES[d][0] == -1)
NORTH = tuple(d for d in range(19) if VELOCITIES[d][1] == 1)
SOUTH = tuple(d for d in range(19) if VELOCITIES[d][1] == -1)
XDIRS = {1: EAST, -1: WEST}
YDIRS = {1: NORTH, -1: SOUTH}
CORNERS = ((1, 1), (-1, -1), (1, -1), (-1, 1))
CORNER_DIR = {(1, 1): 7, (-1, -1): 8, (1, -1): 9, (-1, 1): 10}

CX, CY, NZ = 4, 8, 128
COLS = CX * CY


def dot_product(direction, vector):
    total = None
    for component in range(3):
        factor = VELOCITIES[direction][component]
        if factor != 0:
            term = vector[component] if factor == 1 else -vector[component]
            total = term if total is None else total + term
    return total


def moments(f):
    density = f[0]
    for d in range(1, 19):
        density = density + f[d]
    parts = []
    for component in range(3):
        plus = minus = None
        for d in range(19):
            factor = VELOCITIES[d][component]
            if factor == 1:
                plus = f[d] if plus is None else plus + f[d]
            elif factor == -1:
                minus = f[d] if minus is None else minus + f[d]
        parts.append(plus - minus)
    inverse = 1.0 / density
    return density, inverse, [part * inverse for part in parts]


def collide(f, density, inverse, velocity, field):
    half = 0.5 * inverse
    shifted = [velocity[c] + field[c] * half for c in range(3)]
    squared = shifted[0] * shifted[0] + shifted[1] * shifted[1] + shifted[2] * shifted[2]
    power = shifted[0] * field[0] + shifted[1] * field[1] + shifted[2] * field[2]
    gain = 1.0 - 0.5 * OMEGA
    scaled = OMEGA * density
    base = scaled * (1.0 - 1.5 * squared) - (3.0 * gain) * power
    curved = 4.5 * scaled
    sloped = 3.0 * scaled
    post = [None] * 19
    post[0] = (1.0 - OMEGA) * f[0] + WEIGHTS[0] * base
    for d in range(1, 19, 2):
        s = dot_product(d, shifted)
        g = dot_product(d, field)
        even = base + s * (curved * s + (9.0 * gain) * g)
        odd = sloped * s + (3.0 * gain) * g
        post[d] = (1.0 - OMEGA) * f[d] + WEIGHTS[d] * (even + odd)
        post[d + 1] = (1.0 - OMEGA) * f[d + 1] + WEIGHTS[d] * (even - odd)
    return post


def kernel(
    n_gx,
    n_gy,
    pop_hbm,
    flags_hbm,
    tile_hbm,
    cell_hbm,
    frac_hbm,
    live_hbm,
    target_hbm,
    force_hbm,
    pop_out,
    force_out,
    state,
    post,
    flags_v,
    tile_s,
    cell_v,
    frac_v,
    live_v,
    target_v,
    force_v,
    send_a,
    recv_a,
    send_b,
    recv_b,
    send_r,
    recv_r,
    force_now,
    z_table,
    c_table,
    s_table,
    v_table,
    field_v,
    face_send,
    face_recv,
    edge_send,
    edge_recv,
    corner_send,
    corner_recv,
    force_res,
    in_sem,
    out_sem,
    a_send_sem,
    a_recv_sem,
    b_send_sem,
    b_recv_sem,
    r_send_sem,
    r_recv_sem,
    h_send_sem,
    h_recv_sem,
):
    gx = lax.axis_index("gx")
    gy = lax.axis_index("gy")
    blocks = cell_v.shape[0]

    def around(position, shift, count):
        return lax.rem(position + shift + count, count)

    in_pairs = (
        (tile_hbm, tile_s),
        (cell_hbm, cell_v),
        (frac_hbm, frac_v),
        (live_hbm, live_v),
        (target_hbm, target_v),
        (force_hbm, force_v),
        (pop_hbm, state),
        (flags_hbm, flags_v),
    )
    loads = [
        pltpu.make_async_copy(src, dst, in_sem.at[i]) for i, (src, dst) in enumerate(in_pairs)
    ]
    for load in loads:
        load.start()

    barrier = pltpu.get_barrier_semaphore()

    def greet(step, carry):
        pl.semaphore_signal(
            barrier,
            inc=1,
            device_id={"gx": around(gx, step, n_gx)},
            device_id_type=MESH,
        )
        return carry

    lax.fori_loop(1, n_gx, greet, 0)
    for dx in (-1, 0, 1):
        for dy in (-1, 1):
            pl.semaphore_signal(
                barrier,
                inc=1,
                device_id={"gx": around(gx, dx, n_gx), "gy": around(gy, dy, n_gy)},
                device_id_type=MESH,
            )

    for load in loads[:6]:
        load.wait()

    def pack(t, carry):
        first = jnp.int32(-1)
        second = jnp.int32(-1)
        for b in range(blocks - 1, -1, -1):
            match = tile_s[b, 0] == t
            second = jnp.where(match, first, second)
            first = jnp.where(match, jnp.int32(b), first)
        for s, index in enumerate((first, second)):
            valid = jnp.where(index >= 0, 1.0, 0.0)
            at = jnp.maximum(index, 0)
            send_a[t, 4 * s : 4 * s + 1, :] = cell_v[pl.ds(at, 1), :].astype(jnp.float32)
            send_a[t, 4 * s + 1 : 4 * s + 4, :] = frac_v[at]
            send_b[t, s, 0:3, :] = target_v[at]
            send_b[t, s, 3:6, :] = force_v[at]
            send_b[t, s, 6:7, :] = live_v[pl.ds(at, 1), :].astype(jnp.float32) * valid
            send_b[t, s, 7:8, :] = jnp.zeros((1, NZ), jnp.float32)
        return carry

    lax.fori_loop(0, n_gx, pack, 0)
    recv_a[gx] = send_a[gx]
    recv_b[gx] = send_b[gx]

    pl.semaphore_wait(barrier, n_gx - 1 + 6)

    def copy_a(to, slot):
        return pltpu.make_async_remote_copy(
            src_ref=send_a.at[to],
            dst_ref=recv_a.at[slot],
            send_sem=a_send_sem.at[to],
            recv_sem=a_recv_sem.at[slot],
            device_id={"gx": to},
            device_id_type=MESH,
        )

    def copy_b(to, slot):
        return pltpu.make_async_remote_copy(
            src_ref=send_b.at[to],
            dst_ref=recv_b.at[slot],
            send_sem=b_send_sem.at[to],
            recv_sem=b_recv_sem.at[slot],
            device_id={"gx": to},
            device_id_type=MESH,
        )

    def copy_r(to, slot):
        return pltpu.make_async_remote_copy(
            src_ref=send_r.at[to],
            dst_ref=recv_r.at[slot],
            send_sem=r_send_sem.at[to],
            recv_sem=r_recv_sem.at[slot],
            device_id={"gx": to},
            device_id_type=MESH,
        )

    def each_peer(action):
        def one(step, carry):
            action(around(gx, step, n_gx))
            return carry

        lax.fori_loop(1, n_gx, one, 0)

    each_peer(lambda peer: copy_a(peer, gx).start())
    each_peer(lambda peer: copy_b(peer, gx).start())

    for load in loads[6:]:
        load.wait()

    def velocity_tables():
        f = [state[d] for d in range(19)]
        density, inverse, velocity = moments(f)
        for c in range(3):
            rows = velocity[c].reshape(COLS, NZ)
            high = rows.astype(jnp.bfloat16)
            low = (rows - high.astype(jnp.float32)).astype(jnp.bfloat16)
            for half in range(2):
                v_table[c * COLS : (c + 1) * COLS, half * NZ : (half + 1) * NZ] = high
                v_table[(3 + c) * COLS : (4 + c) * COLS, half * NZ : (half + 1) * NZ] = low

    velocity_tables()

    each_peer(lambda peer: copy_a(gx, peer).wait_recv())

    y_rows = lax.broadcasted_iota(jnp.int32, (CY, NZ), 0)
    z_rows = lax.broadcasted_iota(jnp.int32, (16, NZ), 0)

    def build(src, carry):
        for s in range(SLOT):
            column = pl.ds(pl.multiple_of(src * (SLOT * NZ) + s * NZ, NZ), NZ)
            cell = recv_a[src, 4 * s : 4 * s + 1, :].astype(jnp.int32)
            px = recv_a[src, 4 * s + 1 : 4 * s + 2, :]
            py = recv_a[src, 4 * s + 2 : 4 * s + 3, :]
            pz = recv_a[src, 4 * s + 3 : 4 * s + 4, :]
            i = lax.shift_right_logical(cell, 10)
            j = lax.shift_right_logical(cell, 7) & 7
            k = cell & 127
            wide = (CY, NZ)
            jw = jnp.broadcast_to(j, wide)
            pyw = jnp.broadcast_to(py, wide)
            wy = jnp.where(y_rows == jw, 1.0 - pyw, jnp.where(y_rows == jw + 1, pyw, 0.0))
            for x in range(CX):
                wx = jnp.where(i == x, 1.0 - px, jnp.where(i == x - 1, px, 0.0))
                c_table[x * CY : (x + 1) * CY, column] = jnp.broadcast_to(wx, wide) * wy
            tall = (16, NZ)
            kw = jnp.broadcast_to(k, tall)
            upper = jnp.broadcast_to(pz, tall)
            lower = 1.0 - upper
            upper_high = upper.astype(jnp.bfloat16)
            lower_high = lower.astype(jnp.bfloat16)
            upper_low = (upper - upper_high.astype(jnp.float32)).astype(jnp.bfloat16)
            lower_low = (lower - lower_high.astype(jnp.float32)).astype(jnp.bfloat16)
            k16 = kw.astype(jnp.bfloat16)
            none = jnp.zeros(tall, jnp.bfloat16)
            for chunk in range(NZ // 16):
                here = (z_rows + 16 * chunk).astype(jnp.bfloat16)
                below = (z_rows + (16 * chunk - 1)).astype(jnp.bfloat16)
                is_low = here == k16
                is_up = below == k16
                z_table[16 * chunk : 16 * chunk + 16, column] = jnp.where(
                    is_low, lower_high, jnp.where(is_up, upper_high, none)
                )
                z_table[NZ + 16 * chunk : NZ + 16 * chunk + 16, column] = jnp.where(
                    is_low, lower_low, jnp.where(is_up, upper_low, none)
                )
        return carry

    lax.fori_loop(0, n_gx, build, 0)
    each_peer(lambda peer: copy_b(gx, peer).wait_recv())

    def exchange(step):
        copies = []
        number = 0
        for sx in (1, -1):
            copies.append(
                pltpu.make_async_remote_copy(
                    src_ref=face_send.at[step, 0 if sx == 1 else 1],
                    dst_ref=face_recv.at[step, 0 if sx == 1 else 1],
                    send_sem=h_send_sem.at[step, number],
                    recv_sem=h_recv_sem.at[step, number],
                    device_id={"gx": around(gx, sx, n_gx)},
                    device_id_type=MESH,
                )
            )
            number += 1
        for sy in (1, -1):
            copies.append(
                pltpu.make_async_remote_copy(
                    src_ref=edge_send.at[step, 0 if sy == 1 else 1],
                    dst_ref=edge_recv.at[step, 0 if sy == 1 else 1],
                    send_sem=h_send_sem.at[step, number],
                    recv_sem=h_recv_sem.at[step, number],
                    device_id={"gy": around(gy, sy, n_gy)},
                    device_id_type=MESH,
                )
            )
            number += 1
        for corner, (sx, sy) in enumerate(CORNERS):
            copies.append(
                pltpu.make_async_remote_copy(
                    src_ref=corner_send.at[step, corner],
                    dst_ref=corner_recv.at[step, corner],
                    send_sem=h_send_sem.at[step, number],
                    recv_sem=h_recv_sem.at[step, number],
                    device_id={"gx": around(gx, sx, n_gx), "gy": around(gy, sy, n_gy)},
                    device_id_type=MESH,
                )
            )
            number += 1
        return copies

    flags_f = flags_v[...].astype(jnp.float32)
    for side, sx in enumerate((1, -1)):
        face_send[0, side, 5] = flags_f[CX - 1 if sx == 1 else 0]
    for side, sy in enumerate((1, -1)):
        for x in range(CX):
            y = CY - 1 if sy == 1 else 0
            edge_send[0, side, 20 + x : 21 + x, :] = flags_f[x, y : y + 1, :]
    for corner, (sx, sy) in enumerate(CORNERS):
        x = CX - 1 if sx == 1 else 0
        y = CY - 1 if sy == 1 else 0
        corner_send[0, corner, 0:8, :] = jnp.zeros((8, NZ), jnp.float32)
        corner_send[1, corner, 0:8, :] = jnp.zeros((8, NZ), jnp.float32)
        corner_send[0, corner, 1:2, :] = flags_f[x, y : y + 1, :]

    sublane = lax.broadcasted_iota(jnp.int32, (CY, NZ), 0)

    def pulled(tiles, step, direction, x, dx, dy, dz):
        from_x = x - dx
        if dx != 0 and (from_x < 0 or from_x >= CX):
            side = 0 if dx == 1 else 1
            place = 5 if direction is None else XDIRS[dx].index(direction)
            tile = face_recv[step, side, place]
            outside = True
        else:
            tile = tiles[from_x]
            outside = False
        if dy != 0:
            if outside:
                corner = CORNERS.index((dx, dy))
                row = corner_recv[step, corner, (1 if direction is None else 0) :, :][0:1]
            else:
                side = 0 if dy == 1 else 1
                place = 20 if direction is None else 4 * YDIRS[dy].index(direction)
                row = edge_recv[step, side, place + from_x : place + from_x + 1, :]
            tile = pltpu.roll(tile, 1 if dy == 1 else CY - 1, 0)
            edge = 0 if dy == 1 else CY - 1
            tile = jnp.where(sublane == edge, jnp.broadcast_to(row, (CY, NZ)), tile)
        if dz != 0:
            tile = pltpu.roll(tile, 1 if dz == 1 else NZ - 1, 1)
        return tile

    for step in range(STEPS):
        last = step == STEPS - 1

        def sample(src, carry):
            wide = pl.ds(pl.multiple_of(src * (SLOT * NZ), SLOT * NZ), SLOT * NZ)
            picked = jnp.dot(
                v_table[...], z_table[:, wide], preferred_element_type=jnp.float32
            )
            weights = c_table[:, wide]
            for c in range(3):
                both = (
                    picked[c * COLS : (c + 1) * COLS]
                    + picked[(3 + c) * COLS : (4 + c) * COLS]
                ) * weights
                sampled = jnp.sum(both, axis=0, keepdims=True)
                for s in range(SLOT):
                    lanes = slice(s * NZ, (s + 1) * NZ)
                    live = recv_b[src, s, 6:7, :]
                    target = recv_b[src, s, c : c + 1, :]
                    if step == 0:
                        before = recv_b[src, s, 3 + c : 4 + c, :]
                    else:
                        before = force_now[src, 3 * s + c : 3 * s + c + 1, :]
                    after = before + live * (target - sampled[:, lanes])
                    if last:
                        send_r[src, 3 * s + c : 3 * s + c + 1, :] = after
                    else:
                        force_now[src, 3 * s + c : 3 * s + c + 1, :] = after
                    pushed = weights[:, lanes] * (live * after)
                    column = pl.ds(pl.multiple_of(src * (SLOT * NZ) + s * NZ, NZ), NZ)
                    high = pushed.astype(jnp.bfloat16)
                    low = (pushed - high.astype(jnp.float32)).astype(jnp.bfloat16)
                    s_table[c * COLS : (c + 1) * COLS, column] = high
                    s_table[(3 + c) * COLS : (4 + c) * COLS, column] = low
            if last:
                send_r[src, 6:8, :] = jnp.zeros((2, NZ), jnp.float32)
            return carry

        lax.fori_loop(0, n_gx, sample, 0)
        if last:
            recv_r[gx] = send_r[gx]
            each_peer(lambda peer: copy_r(peer, gx).start())

        spread = lax.dot_general(
            s_table[...],
            z_table[...],
            (((1,), (1,)), ((), ())),
            preferred_element_type=jnp.float32,
        )
        field = (spread[: 3 * COLS, :NZ] + spread[3 * COLS :, :NZ]) + (
            spread[: 3 * COLS, NZ:] + spread[3 * COLS :, NZ:]
        )
        field = field.reshape(3, CX, CY, NZ)
        f = [state[d] for d in range(19)]
        density, inverse, velocity = moments(f)
        after = collide(f, density, inverse, velocity, [field[c] for c in range(3)])
        for side, sx in enumerate((1, -1)):
            for place, d in enumerate(XDIRS[sx]):
                face_send[step, side, place] = after[d][CX - 1 if sx == 1 else 0]
        for side, sy in enumerate((1, -1)):
            y = CY - 1 if sy == 1 else 0
            for place, d in enumerate(YDIRS[sy]):
                for x in range(CX):
                    row = 4 * place + x
                    edge_send[step, side, row : row + 1, :] = after[d][x, y : y + 1, :]
        for corner, (sx, sy) in enumerate(CORNERS):
            x = CX - 1 if sx == 1 else 0
            y = CY - 1 if sy == 1 else 0
            corner_send[step, corner, 0:1, :] = after[CORNER_DIR[sx, sy]][x, y : y + 1, :]
        if step > 0:
            for side in range(2):
                face_send[step, side, 5] = jnp.zeros((CY, NZ), jnp.float32)
                edge_send[step, side, 20:24, :] = jnp.zeros((4, NZ), jnp.float32)
        copies = exchange(step)
        for copy in copies:
            copy.start()
        for d in range(19):
            post[d] = after[d]
        if last:
            each_peer(lambda peer: copy_r(gx, peer).wait_recv())
            for b in range(blocks):
                tile = tile_s[b, 0]
                rank = jnp.int32(0)
                for other in range(b):
                    rank = rank + jnp.where(tile_s[other, 0] == tile, 1, 0)
                whole = recv_r[tile]
                force_res[b] = jnp.where(rank == 0, whole[0:3], whole[3:6])
            force_copy = pltpu.make_async_copy(force_res, force_out, out_sem.at[0])
            force_copy.start()
        for copy in copies:
            copy.wait_recv()
        tiles_flag = [flags_v[x].astype(jnp.float32) for x in range(CX)]
        for d in range(19):
            dx, dy, dz = VELOCITIES[d]
            tiles = [post[d, x] for x in range(CX)]
            for x in range(CX):
                solid = pulled(tiles_flag, 0, None, x, dx, dy, dz)
                moved = pulled(tiles, step, d, x, dx, dy, dz)
                state[d, x] = jnp.where(solid == 1.0, post[OPPOSITE[d], x], moved)
        if not last:
            velocity_tables()
        for copy in copies:
            copy.wait_send()

    state_copy = pltpu.make_async_copy(state, pop_out, out_sem.at[1])
    state_copy.start()
    each_peer(lambda peer: copy_a(peer, gx).wait_send())
    each_peer(lambda peer: copy_b(peer, gx).wait_send())
    each_peer(lambda peer: copy_r(peer, gx).wait_send())
    force_copy.wait()
    state_copy.wait()


def body(
    populations,
    flags,
    block_tile,
    marker_cell,
    marker_frac,
    marker_live,
    marker_target,
    marker_force,
):
    n_gx = lax.axis_size("gx")
    n_gy = lax.axis_size("gy")
    blocks, markers = marker_cell.shape
    width = n_gx * SLOT * markers
    f32, bf16, i32 = jnp.float32, jnp.bfloat16, jnp.int32
    dma = pltpu.SemaphoreType.DMA
    vmem = pltpu.VMEM
    anywhere = pl.BlockSpec(memory_space=pl.ANY)
    return pl.pallas_call(
        functools.partial(kernel, n_gx, n_gy),
        out_shape=(
            jax.ShapeDtypeStruct(populations.shape, f32),
            jax.ShapeDtypeStruct(marker_force.shape, f32),
        ),
        in_specs=[anywhere] * 8,
        out_specs=(anywhere, anywhere),
        scratch_shapes=[
            vmem(populations.shape, f32),
            vmem(populations.shape, f32),
            vmem(flags.shape, i32),
            pltpu.SMEM(block_tile.shape, i32),
            vmem(marker_cell.shape, i32),
            vmem(marker_frac.shape, f32),
            vmem(marker_live.shape, i32),
            vmem(marker_target.shape, f32),
            vmem(marker_force.shape, f32),
            vmem((n_gx, 8, markers), f32),
            vmem((n_gx, 8, markers), f32),
            vmem((n_gx, SLOT, 8, markers), f32),
            vmem((n_gx, SLOT, 8, markers), f32),
            vmem((n_gx, 8, markers), f32),
            vmem((n_gx, 8, markers), f32),
            vmem((n_gx, 8, markers), f32),
            vmem((2 * NZ, width), bf16),
            vmem((COLS, width), f32),
            vmem((6 * COLS, width), bf16),
            vmem((6 * COLS, 2 * NZ), bf16),
            vmem((3, CX, CY, NZ), f32),
            vmem((STEPS, 2, 6, CY, NZ), f32),
            vmem((STEPS, 2, 6, CY, NZ), f32),
            vmem((STEPS, 2, 24, NZ), f32),
            vmem((STEPS, 2, 24, NZ), f32),
            vmem((STEPS, 4, 8, NZ), f32),
            vmem((STEPS, 4, 8, NZ), f32),
            vmem(marker_force.shape, f32),
            dma((8,)),
            dma((2,)),
            dma((n_gx,)),
            dma((n_gx,)),
            dma((n_gx,)),
            dma((n_gx,)),
            dma((n_gx,)),
            dma((n_gx,)),
            dma((STEPS, 8)),
            dma((STEPS, 8)),
        ],
        compiler_params=pltpu.CompilerParams(
            collective_id=0,
            has_side_effects=True,
            vmem_limit_bytes=32 * 1024 * 1024,
        ),
    )(
        populations,
        flags,
        block_tile,
        marker_cell,
        marker_frac,
        marker_live,
        marker_target,
        marker_force,
    )


def solution(mesh):
    in_specs = (
        P(None, "gx", "gy", None),
        P("gx", "gy", None),
        P(("gx", "gy"), None),
        P(("gx", "gy"), None),
        P(("gx", "gy"), None, None),
        P(("gx", "gy"), None),
        P(("gx", "gy"), None, None),
        P(("gx", "gy"), None, None),
    )
    out_specs = (P(None, "gx", "gy", None), P(("gx", "gy"), None, None))
    return jax.shard_map(body, mesh=mesh, in_specs=in_specs, out_specs=out_specs, check_vma=False)
```

```python
import functools

import jax
import jax.numpy as jnp
from jax import lax
from jax.experimental import pallas as pl
from jax.experimental.pallas import tpu as pltpu
from jax.sharding import PartitionSpec as P

STEPS = 2
SLOT = 2
MESH = pl.DeviceIdType.MESH

VELOCITIES = (
    (0, 0, 0),
    (1, 0, 0),
    (-1, 0, 0),
    (0, 1, 0),
    (0, -1, 0),
    (0, 0, 1),
    (0, 0, -1),
    (1, 1, 0),
    (-1, -1, 0),
    (1, -1, 0),
    (-1, 1, 0),
    (1, 0, 1),
    (-1, 0, -1),
    (1, 0, -1),
    (-1, 0, 1),
    (0, 1, 1),
    (0, -1, -1),
    (0, 1, -1),
    (0, -1, 1),
)
OPPOSITE = (0, 2, 1, 4, 3, 6, 5, 8, 7, 10, 9, 12, 11, 14, 13, 16, 15, 18, 17)
WEIGHTS = (1.0 / 3.0,) + (1.0 / 18.0,) * 6 + (1.0 / 36.0,) * 12
OMEGA = 1.25

EAST = tuple(d for d in range(19) if VELOCITIES[d][0] == 1)
WEST = tuple(d for d in range(19) if VELOCITIES[d][0] == -1)
NORTH = tuple(d for d in range(19) if VELOCITIES[d][1] == 1)
SOUTH = tuple(d for d in range(19) if VELOCITIES[d][1] == -1)
XDIRS = {1: EAST, -1: WEST}
YDIRS = {1: NORTH, -1: SOUTH}
CORNERS = ((1, 1), (-1, -1), (1, -1), (-1, 1))
CORNER_DIR = {(1, 1): 7, (-1, -1): 8, (1, -1): 9, (-1, 1): 10}

NEIGHBOURS = ((1, 0), (-1, 0), (0, 1), (0, -1)) + CORNERS
GROUPS = 4

CX, CY, NZ = 4, 8, 128
COLS = CX * CY


def dot_product(direction, vector):
    total = None
    for component in range(3):
        factor = VELOCITIES[direction][component]
        if factor != 0:
            term = vector[component] if factor == 1 else -vector[component]
            total = term if total is None else total + term
    return total


def moments(f):
    density = f[0]
    for d in range(1, 19):
        density = density + f[d]
    parts = []
    for component in range(3):
        plus = minus = None
        for d in range(19):
            factor = VELOCITIES[d][component]
            if factor == 1:
                plus = f[d] if plus is None else plus + f[d]
            elif factor == -1:
                minus = f[d] if minus is None else minus + f[d]
        parts.append(plus - minus)
    inverse = 1.0 / density
    return density, inverse, [part * inverse for part in parts]


def collide(f, density, inverse, velocity, field):
    half = 0.5 * inverse
    shifted = [velocity[c] + field[c] * half for c in range(3)]
    squared = shifted[0] * shifted[0] + shifted[1] * shifted[1] + shifted[2] * shifted[2]
    power = shifted[0] * field[0] + shifted[1] * field[1] + shifted[2] * field[2]
    gain = 1.0 - 0.5 * OMEGA
    scaled = OMEGA * density
    base = scaled * (1.0 - 1.5 * squared) - (3.0 * gain) * power
    curved = 4.5 * scaled
    sloped = 3.0 * scaled
    post = [None] * 19
    post[0] = (1.0 - OMEGA) * f[0] + WEIGHTS[0] * base
    for d in range(1, 19, 2):
        s = dot_product(d, shifted)
        g = dot_product(d, field)
        even = base + s * (curved * s + (9.0 * gain) * g)
        odd = sloped * s + (3.0 * gain) * g
        post[d] = (1.0 - OMEGA) * f[d] + WEIGHTS[d] * (even + odd)
        post[d + 1] = (1.0 - OMEGA) * f[d + 1] + WEIGHTS[d] * (even - odd)
    return post


def offsets(count):
    order = [0]
    for step in range(1, count // 2 + 1):
        order.append(step)
        if 2 * step != count:
            order.append(-step)
    return order


def kernel(
    n_gx,
    n_gy,
    pop_hbm,
    flags_hbm,
    tile_hbm,
    cell_hbm,
    frac_hbm,
    live_hbm,
    target_hbm,
    force_hbm,
    pop_out,
    force_out,
    state,
    post,
    moment_v,
    flags_v,
    tile_s,
    cell_v,
    frac_v,
    live_v,
    target_v,
    force_v,
    push_v,
    pull_v,
    send_a,
    recv_a,
    send_b,
    recv_b,
    send_c,
    recv_c,
    send_r,
    recv_r,
    force_now,
    sample_v,
    z_table,
    zt_table,
    c_table,
    s_table,
    v_table,
    solid_v,
    solid_row,
    back_row,
    flag_send,
    flag_recv,
    face_send,
    face_recv,
    edge_send,
    edge_recv,
    corner_send,
    corner_recv,
    in_sem,
    a_send_sem,
    a_recv_sem,
    b_send_sem,
    b_recv_sem,
    c_send_sem,
    c_recv_sem,
    r_send_sem,
    r_recv_sem,
    f_send_sem,
    f_recv_sem,
    h_send_sem,
    h_recv_sem,
):
    gx = lax.axis_index("gx")
    gy = lax.axis_index("gy")
    blocks = cell_v.shape[0]
    near = offsets(n_gx)
    place_of = {off % n_gx: n for n, off in enumerate(near)}
    far_first = list(range(n_gx - 1, 0, -1))

    def around(position, shift, count):
        return lax.rem(position + (shift + count), count)

    def device(dx, dy):
        if dy == 0:
            return {"gx": around(gx, dx, n_gx)}
        if dx == 0:
            return {"gy": around(gy, dy, n_gy)}
        return {"gx": around(gx, dx, n_gx), "gy": around(gy, dy, n_gy)}

    barrier = pltpu.get_barrier_semaphore()
    for n in far_first:
        pl.semaphore_signal(barrier, inc=1, device_id=device(near[n], 0), device_id_type=MESH)
    for dx, dy in NEIGHBOURS:
        if dy != 0:
            pl.semaphore_signal(barrier, inc=1, device_id=device(dx, dy), device_id_type=MESH)

    in_pairs = (
        (tile_hbm, tile_s),
        (cell_hbm, cell_v),
        (frac_hbm, frac_v),
        (live_hbm, live_v),
        (target_hbm, target_v),
        (force_hbm, force_v),
        (pop_hbm, state),
        (flags_hbm, flags_v),
    )
    loads = [
        pltpu.make_async_copy(src, dst, in_sem.at[i]) for i, (src, dst) in enumerate(in_pairs)
    ]
    for load in loads:
        load.start()
    for load in loads[:6]:
        load.wait()

    alive = live_v[...].astype(jnp.float32)
    for c in range(3):
        pull_v[c] = alive * target_v[c]
        push_v[c] = alive * (force_v[c] + target_v[c])

    def pack(t, carry):
        first = jnp.int32(-1)
        second = jnp.int32(-1)
        for b in range(blocks - 1, -1, -1):
            match = tile_s[0, b] == t
            second = jnp.where(match, first, second)
            first = jnp.where(match, jnp.int32(b), first)
        for s, index in enumerate((first, second)):
            valid = jnp.where(index >= 0, 1.0, 0.0)
            at = pl.ds(jnp.maximum(index, 0), 1)
            send_a[t, 4 * s : 4 * s + 1, :] = cell_v[at, :].astype(jnp.float32)
            for c in range(3):
                send_a[t, 4 * s + 1 + c : 4 * s + 2 + c, :] = frac_v[c, at, :]
                send_b[t, 4 * s + c : 4 * s + c + 1, :] = push_v[c, at, :] * valid
                send_c[t, 3 * s + c : 3 * s + c + 1, :] = pull_v[c, at, :] * valid
            send_b[t, 4 * s + 3 : 4 * s + 4, :] = live_v[at, :].astype(jnp.float32) * valid
        return carry

    lax.fori_loop(0, n_gx, pack, 0)
    recv_a[0] = send_a[gx]
    recv_b[0] = send_b[gx]
    recv_c[0] = send_c[gx]

    loads[7].wait()
    for number, (dx, dy) in enumerate(NEIGHBOURS):
        x = CX - 1 if dx == 1 else 0
        y = CY - 1 if dy == 1 else 0
        if dy == 0:
            flag_send[number] = flags_v[x].astype(jnp.float32)
        elif dx == 0:
            for x in range(CX):
                flag_send[number, x : x + 1, :] = flags_v[x, y : y + 1, :].astype(jnp.float32)
        else:
            flag_send[number, 0:1, :] = flags_v[x, y : y + 1, :].astype(jnp.float32)

    def peer_copy(send, recv, send_sem, recv_sem, rows=8):
        def copy(n):
            back = place_of[-near[n] % n_gx]
            return pltpu.make_async_remote_copy(
                src_ref=send.at[around(gx, near[n], n_gx), 0:rows],
                dst_ref=recv.at[back, 0:rows],
                send_sem=send_sem.at[n],
                recv_sem=recv_sem.at[back],
                device_id=device(near[n], 0),
                device_id_type=MESH,
            )

        return {n: copy(n) for n in far_first}

    def opposite(n):
        return place_of[-near[n] % n_gx]

    copies_a = peer_copy(send_a, recv_a, a_send_sem, a_recv_sem)
    copies_b = peer_copy(send_b, recv_b, b_send_sem, b_recv_sem)
    copies_c = peer_copy(send_c, recv_c, c_send_sem, c_recv_sem, 6)
    copies_r = {
        n: pltpu.make_async_remote_copy(
            src_ref=send_r.at[n, 0:6],
            dst_ref=recv_r.at[gx, 0:6],
            send_sem=r_send_sem.at[n],
            recv_sem=r_recv_sem.at[opposite(n)],
            device_id=device(near[n], 0),
            device_id_type=MESH,
        )
        for n in far_first
    }
    flag_rows = (CY, CY, CX, CX, 1, 1, 1, 1)
    copies_f = [
        pltpu.make_async_remote_copy(
            src_ref=flag_send.at[number, 0 : flag_rows[number]],
            dst_ref=flag_recv.at[number, 0 : flag_rows[number]],
            send_sem=f_send_sem.at[number],
            recv_sem=f_recv_sem.at[number],
            device_id=device(dx, dy),
            device_id_type=MESH,
        )
        for number, (dx, dy) in enumerate(NEIGHBOURS)
    ]

    pl.semaphore_wait(barrier, n_gx - 1 + 6)
    for n in far_first:
        copies_a[n].start()
    for n in far_first:
        copies_b[n].start()
    for copy in copies_f:
        copy.start()

    loads[6].wait()

    def velocity_tables(f):
        density, inverse, velocity = moments(f)
        moment_v[0] = density
        moment_v[1] = inverse
        for c in range(3):
            moment_v[2 + c] = velocity[c]
            rows = velocity[c].reshape(COLS, NZ)
            high = rows.astype(jnp.bfloat16)
            low = (rows - high.astype(jnp.float32)).astype(jnp.bfloat16)
            for half in range(2):
                v_table[c * COLS : (c + 1) * COLS, half * NZ : (half + 1) * NZ] = high
                v_table[(3 + c) * COLS : (4 + c) * COLS, half * NZ : (half + 1) * NZ] = low

    velocity_tables([state[d] for d in range(19)])

    y_rows = lax.broadcasted_iota(jnp.int32, (CY, NZ), 0)
    z_rows = lax.broadcasted_iota(jnp.int32, (16, NZ), 0)

    def build(n):
        for s in range(SLOT):
            begin = (n * SLOT + s) * NZ
            column = slice(begin, begin + NZ)
            cell = recv_a[n, 4 * s : 4 * s + 1, :].astype(jnp.int32)
            px = recv_a[n, 4 * s + 1 : 4 * s + 2, :]
            py = recv_a[n, 4 * s + 2 : 4 * s + 3, :]
            pz = recv_a[n, 4 * s + 3 : 4 * s + 4, :]
            i = lax.shift_right_logical(cell, 10)
            j = lax.shift_right_logical(cell, 7) & 7
            k = cell & 127
            wide = (CY, NZ)
            jw = jnp.broadcast_to(j, wide)
            pyw = jnp.broadcast_to(py, wide)
            wy = jnp.where(y_rows == jw, 1.0 - pyw, jnp.where(y_rows == jw + 1, pyw, 0.0))
            for x in range(CX):
                wx = jnp.where(i == x, 1.0 - px, jnp.where(i == x - 1, px, 0.0))
                c_table[x * CY : (x + 1) * CY, column] = jnp.broadcast_to(wx, wide) * wy
            tall = (16, NZ)
            kw = jnp.broadcast_to(k, tall)
            upper = jnp.broadcast_to(pz, tall)
            lower = 1.0 - upper
            upper_high = upper.astype(jnp.bfloat16)
            lower_high = lower.astype(jnp.bfloat16)
            upper_low = (upper - upper_high.astype(jnp.float32)).astype(jnp.bfloat16)
            lower_low = (lower - lower_high.astype(jnp.float32)).astype(jnp.bfloat16)
            k16 = kw.astype(jnp.bfloat16)
            none = jnp.zeros(tall, jnp.bfloat16)
            for chunk in range(NZ // 16):
                here = (z_rows + 16 * chunk).astype(jnp.bfloat16)
                below = (z_rows + (16 * chunk - 1)).astype(jnp.bfloat16)
                is_low = here == k16
                is_up = below == k16
                z_table[16 * chunk : 16 * chunk + 16, column] = jnp.where(
                    is_low, lower_high, jnp.where(is_up, upper_high, none)
                )
                z_table[NZ + 16 * chunk : NZ + 16 * chunk + 16, column] = jnp.where(
                    is_low, lower_low, jnp.where(is_up, upper_low, none)
                )

    def sample(n):
        wide = slice(n * SLOT * NZ, (n + 1) * SLOT * NZ)
        picked = jnp.dot(v_table[...], z_table[:, wide], preferred_element_type=jnp.float32)
        weights = c_table[:, wide]
        for c in range(3):
            both = (
                picked[c * COLS : (c + 1) * COLS] + picked[(3 + c) * COLS : (4 + c) * COLS]
            ) * weights
            sampled = jnp.sum(both, axis=0, keepdims=True)
            for s in range(SLOT):
                sample_v[n, 3 * s + c : 3 * s + c + 1, :] = sampled[:, s * NZ : (s + 1) * NZ]

    def push(n, step):
        for s in range(SLOT):
            rows = slice(3 * s, 3 * s + 3)
            column = slice((n * SLOT + s) * NZ, (n * SLOT + s + 1) * NZ)
            live = recv_b[n, 4 * s + 3 : 4 * s + 4, :]
            if step == 0:
                before = recv_b[n, 4 * s : 4 * s + 3, :]
            else:
                before = force_now[n, rows, :] + recv_c[n, rows, :]
            pushed = before - live * sample_v[n, rows, :]
            into = send_r if step == STEPS - 1 else force_now
            into[n, rows, :] = pushed
            for c in range(3):
                spread_row = c_table[:, column] * pushed[c : c + 1]
                high = spread_row.astype(jnp.bfloat16)
                low = (spread_row - high.astype(jnp.float32)).astype(jnp.bfloat16)
                s_table[c * COLS : (c + 1) * COLS, column] = high
                s_table[(3 + c) * COLS : (4 + c) * COLS, column] = low

    def spread(members, step):
        wide = slice(members[0] * SLOT * NZ, (members[-1] + 1) * SLOT * NZ)
        if step > 0:
            return jnp.dot(
                s_table[:, wide], zt_table[wide, :], preferred_element_type=jnp.float32
            )
        return lax.dot_general(
            s_table[:, wide],
            z_table[:, wide],
            (((1,), (1,)), ((), ())),
            preferred_element_type=jnp.float32,
        )

    def turn_table():
        for block in range(n_gx * SLOT):
            for half in range(2):
                zt_table[block * NZ : (block + 1) * NZ, half * NZ : (half + 1) * NZ] = z_table[
                    half * NZ : (half + 1) * NZ, block * NZ : (block + 1) * NZ
                ].T

    def rim_copies(step):
        def copy(number, src, dst):
            return pltpu.make_async_remote_copy(
                src_ref=src,
                dst_ref=dst,
                send_sem=h_send_sem.at[step, number],
                recv_sem=h_recv_sem.at[step, number],
                device_id=device(*NEIGHBOURS[number]),
                device_id_type=MESH,
            )

        out = []
        for number in range(8):
            if number < 2:
                out.append(
                    copy(number, face_send.at[step, number], face_recv.at[step, number])
                )
            elif number < 4:
                out.append(
                    copy(
                        number,
                        edge_send.at[step, number - 2, 0:20],
                        edge_recv.at[step, number - 2, 0:20],
                    )
                )
            else:
                out.append(
                    copy(
                        number,
                        corner_send.at[step, number - 4, 0:1],
                        corner_recv.at[step, number - 4, 0:1],
                    )
                )
        return out

    def shifted(tile, dy, dz):
        if dy != 0:
            tile = pltpu.roll(tile, 1 if dy == 1 else CY - 1, 0)
        if dz != 0:
            tile = pltpu.roll(tile, 1 if dz == 1 else NZ - 1, 1)
        return tile

    def solid_masks():
        tiles = [flags_v[x].astype(jnp.float32) for x in range(CX)]
        sublane = lax.broadcasted_iota(jnp.int32, (CY, NZ), 0)
        for d in range(1, 19):
            dx, dy, dz = VELOCITIES[d]
            for x in range(CX):
                from_x = x - dx
                outside = from_x < 0 or from_x >= CX
                if outside:
                    tile = flag_recv[NEIGHBOURS.index((dx, 0))]
                else:
                    tile = tiles[from_x]
                if dy != 0:
                    if outside:
                        row = flag_recv[NEIGHBOURS.index((dx, dy)), 0:1, :]
                    else:
                        row = flag_recv[NEIGHBOURS.index((0, dy)), from_x : from_x + 1, :]
                    edge = 0 if dy == 1 else CY - 1
                    tile = jnp.where(
                        sublane == edge, jnp.broadcast_to(row, (CY, NZ)), shifted(tile, dy, 0)
                    )
                solid_v[d, x] = shifted(tile, 0, dz)
        for side, sy in enumerate((1, -1)):
            y = 0 if sy == 1 else CY - 1
            solid_row[side] = jnp.zeros((24, NZ), jnp.float32)
            back_row[side] = jnp.zeros((24, NZ), jnp.float32)
            for place, d in enumerate(YDIRS[sy]):
                for from_x in range(CX):
                    x = from_x + VELOCITIES[d][0]
                    if 0 <= x < CX:
                        row = 4 * place + from_x
                        solid_row[side, row : row + 1, :] = solid_v[d, x, y : y + 1, :]

    def stream_inside(into):
        into[0] = post[0]
        for d in range(1, 19):
            dx, dy, dz = VELOCITIES[d]
            for x in range(CX):
                if 0 <= x - dx < CX:
                    moved = shifted(post[d, x - dx], dy, dz)
                    into[d, x] = jnp.where(solid_v[d, x] == 1.0, post[OPPOSITE[d], x], moved)
        for side, sy in enumerate((1, -1)):
            y = 0 if sy == 1 else CY - 1
            for place, d in enumerate(YDIRS[sy]):
                for from_x in range(CX):
                    x = from_x + VELOCITIES[d][0]
                    if 0 <= x < CX:
                        row = 4 * place + from_x
                        back_row[side, row : row + 1, :] = post[OPPOSITE[d], x, y : y + 1, :]

    def stream_edge(into, step, side):
        sy = (1, -1)[side]
        y = 0 if sy == 1 else CY - 1
        dirs = YDIRS[sy]
        half = lax.broadcasted_iota(jnp.int32, (8, NZ), 0) < 4
        parts = [edge_recv[step, side, 8 * p : 8 * p + (4 if p == 2 else 8), :] for p in range(3)]
        parts[1] = jnp.where(half, parts[1], shifted(parts[1], 0, VELOCITIES[dirs[3]][2]))
        parts[2] = shifted(parts[2], 0, VELOCITIES[dirs[4]][2])
        parts = [
            jnp.where(
                solid_row[side, 8 * p : 8 * p + parts[p].shape[0], :] == 1.0,
                back_row[side, 8 * p : 8 * p + parts[p].shape[0], :],
                parts[p],
            )
            for p in range(3)
        ]
        for place, d in enumerate(dirs):
            for from_x in range(CX):
                x = from_x + VELOCITIES[d][0]
                if 0 <= x < CX:
                    row = 4 * place + from_x
                    into[d, x, y : y + 1, :] = parts[row // 8][row % 8 : row % 8 + 1, :]

    def stream_face(into, step, side):
        sx = (1, -1)[side]
        x = 0 if sx == 1 else CX - 1
        for place, d in enumerate(XDIRS[sx]):
            _, dy, dz = VELOCITIES[d]
            moved = shifted(face_recv[step, side, place], dy, dz)
            into[d, x] = jnp.where(solid_v[d, x] == 1.0, post[OPPOSITE[d], x], moved)

    def stream_corner(into, step, corner):
        sx, sy = CORNERS[corner]
        d = CORNER_DIR[sx, sy]
        x = 0 if sx == 1 else CX - 1
        y = slice(0, 1) if sy == 1 else slice(CY - 1, CY)
        into[d, x, y, :] = jnp.where(
            solid_v[d, x, y, :] == 1.0,
            post[OPPOSITE[d], x, y, :],
            corner_recv[step, corner, 0:1, :],
        )

    per = n_gx // GROUPS
    groups = [list(range(g * per, (g + 1) * per)) for g in range(GROUPS)]
    all_rims = []
    for step in range(STEPS):
        last = step == STEPS - 1
        total = None
        if step == 0:
            for members in groups:
                for n in members:
                    if n > 0:
                        copies_a[opposite(n)].wait_recv()
                for n in members:
                    build(n)
                for n in members:
                    sample(n)
        for members in groups:
            if step == 0:
                for n in members:
                    if n > 0:
                        copies_b[opposite(n)].wait_recv()
            else:
                for n in members:
                    sample(n)
                if members is groups[0]:
                    for n in far_first:
                        copies_c[opposite(n)].wait_recv()
            for n in members:
                push(n, step)
            if members is groups[-1]:
                if step == 0:
                    for n in far_first:
                        copies_c[n].start()
                if last:
                    recv_r[gx] = send_r[0]
                    for n in far_first:
                        copies_r[n].start()
            part = spread(members, step)
            total = part if total is None else total + part
        field = (total[: 3 * COLS, :NZ] + total[3 * COLS :, :NZ]) + (
            total[: 3 * COLS, NZ:] + total[3 * COLS :, NZ:]
        )
        field = field.reshape(3, CX, CY, NZ)
        f = [state[d] for d in range(19)]
        after = collide(
            f,
            moment_v[0],
            moment_v[1],
            [moment_v[2 + c] for c in range(3)],
            [field[c] for c in range(3)],
        )
        copies = rim_copies(step)
        for corner, (sx, sy) in enumerate(CORNERS):
            x = CX - 1 if sx == 1 else 0
            y = CY - 1 if sy == 1 else 0
            corner_send[step, corner, 0:1, :] = after[CORNER_DIR[sx, sy]][x, y : y + 1, :]
        for side, sx in enumerate((1, -1)):
            for place, d in enumerate(XDIRS[sx]):
                face_send[step, side, place] = after[d][CX - 1 if sx == 1 else 0]
        for side, sy in enumerate((1, -1)):
            y = CY - 1 if sy == 1 else 0
            for place, d in enumerate(YDIRS[sy]):
                for x in range(CX):
                    row = 4 * place + x
                    edge_send[step, side, row : row + 1, :] = after[d][x, y : y + 1, :]
        for number in (4, 5, 6, 7, 0, 1, 2, 3):
            copies[number].start()
        for d in range(19):
            post[d] = after[d]
        into = pop_out if last else state
        if step == 0:
            for copy in copies_f:
                copy.wait_recv()
            turn_table()
            solid_masks()
        stream_inside(into)
        for side in range(2):
            copies[2 + side].wait_recv()
            stream_edge(into, step, side)
        if last:
            for n in far_first:
                copies_r[opposite(n)].wait_recv()
            for b in range(blocks):
                tile = tile_s[0, b]
                rank = jnp.int32(0)
                for other in range(b):
                    rank = rank + jnp.where(tile_s[0, other] == tile, 1, 0)
                half = jnp.where(rank == 0, recv_r[tile, 0:3, :], recv_r[tile, 3:6, :])
                for c in range(3):
                    push_v[c, b : b + 1, :] = half[c : c + 1]
            keep = live_v[...] == 1
            for c in range(3):
                force_out[c] = jnp.where(keep, push_v[c], force_v[c])
        for side in range(2):
            copies[side].wait_recv()
            stream_face(into, step, side)
        for corner in range(4):
            copies[4 + corner].wait_recv()
            stream_corner(into, step, corner)
        if not last:
            velocity_tables([state[d] for d in range(19)])
        all_rims += copies

    for group in (copies_a, copies_b, copies_c, copies_r):
        for n in far_first:
            group[n].wait_send()
    for copy in copies_f + all_rims:
        copy.wait_send()


def deliver(state, force, state_out, force_out, sem):
    copies = [
        pltpu.make_async_copy(state, state_out, sem.at[0]),
        pltpu.make_async_copy(force, force_out, sem.at[1]),
    ]
    for copy in copies:
        copy.start()
    for copy in copies:
        copy.wait()


def body(
    populations,
    flags,
    block_tile,
    marker_cell,
    marker_frac,
    marker_live,
    marker_target,
    marker_force,
):
    n_gx = lax.axis_size("gx")
    n_gy = lax.axis_size("gy")
    blocks, markers = marker_cell.shape
    width = n_gx * SLOT * markers
    marker_rows = (3, blocks, markers)
    packed = (n_gx, 8, markers)
    f32, bf16, i32 = jnp.float32, jnp.bfloat16, jnp.int32
    dma = pltpu.SemaphoreType.DMA
    vmem = pltpu.VMEM
    in_hbm = functools.partial(pltpu.with_memory_space_constraint, memory_space=pltpu.HBM)
    in_vmem = functools.partial(pltpu.with_memory_space_constraint, memory_space=pltpu.VMEM)
    anywhere = pl.BlockSpec(memory_space=pl.ANY)
    inside = pl.BlockSpec(memory_space=pltpu.VMEM)
    state, force = pl.pallas_call(
        functools.partial(kernel, n_gx, n_gy),
        out_shape=(vmem(populations.shape, f32), vmem(marker_rows, f32)),
        in_specs=[anywhere] * 8,
        out_specs=(inside, inside),
        scratch_shapes=[
            vmem(populations.shape, f32),
            vmem(populations.shape, f32),
            vmem((5, CX, CY, NZ), f32),
            vmem(flags.shape, i32),
            pltpu.SMEM((1, blocks), i32),
            vmem(marker_cell.shape, i32),
            vmem(marker_rows, f32),
            vmem(marker_live.shape, i32),
            vmem(marker_rows, f32),
            vmem(marker_rows, f32),
            vmem(marker_rows, f32),
            vmem(marker_rows, f32),
        ]
        + [vmem(packed, f32)] * 10
        + [
            vmem((2 * NZ, width), bf16),
            vmem((width, 2 * NZ), bf16),
            vmem((COLS, width), f32),
            vmem((6 * COLS, width), bf16),
            vmem((6 * COLS, 2 * NZ), bf16),
            vmem(populations.shape, f32),
            vmem((2, 24, NZ), f32),
            vmem((2, 24, NZ), f32),
            vmem((8, CY, NZ), f32),
            vmem((8, CY, NZ), f32),
            vmem((STEPS, 2, 5, CY, NZ), f32),
            vmem((STEPS, 2, 5, CY, NZ), f32),
            vmem((STEPS, 2, 24, NZ), f32),
            vmem((STEPS, 2, 24, NZ), f32),
            vmem((STEPS, 4, 8, NZ), f32),
            vmem((STEPS, 4, 8, NZ), f32),
            dma((8,)),
        ]
        + [dma((n_gx,))] * 8
        + [dma((8,))] * 2
        + [dma((STEPS, 8))] * 2,
        compiler_params=pltpu.CompilerParams(
            collective_id=0,
            has_side_effects=True,
            vmem_limit_bytes=32 * 1024 * 1024,
        ),
    )(
        in_hbm(populations),
        in_hbm(flags),
        in_hbm(block_tile.T),
        in_hbm(marker_cell),
        in_hbm(marker_frac.transpose(1, 0, 2)),
        in_hbm(marker_live),
        in_hbm(marker_target.transpose(1, 0, 2)),
        in_hbm(marker_force.transpose(1, 0, 2)),
    )
    state, force = pl.pallas_call(
        deliver,
        out_shape=(
            jax.ShapeDtypeStruct(populations.shape, f32),
            jax.ShapeDtypeStruct(marker_rows, f32),
        ),
        in_specs=[inside] * 2,
        out_specs=(anywhere, anywhere),
        scratch_shapes=[dma((2,))],
    )(in_vmem(state), in_vmem(force))
    return state, force.transpose(1, 0, 2)


def solution(mesh):
    in_specs = (
        P(None, "gx", "gy", None),
        P("gx", "gy", None),
        P(("gx", "gy"), None),
        P(("gx", "gy"), None),
        P(("gx", "gy"), None, None),
        P(("gx", "gy"), None),
        P(("gx", "gy"), None, None),
        P(("gx", "gy"), None, None),
    )
    out_specs = (P(None, "gx", "gy", None), P(("gx", "gy"), None, None))
    return jax.shard_map(body, mesh=mesh, in_specs=in_specs, out_specs=out_specs, check_vma=False)
```

```python
import functools

import jax
import jax.numpy as jnp
from jax import lax
from jax.experimental import pallas as pl
from jax.experimental.pallas import tpu as pltpu
from jax.sharding import PartitionSpec as P

STEPS = 2
SLOT = 2
MESH = pl.DeviceIdType.MESH

VELOCITIES = (
    (0, 0, 0),
    (1, 0, 0),
    (-1, 0, 0),
    (0, 1, 0),
    (0, -1, 0),
    (0, 0, 1),
    (0, 0, -1),
    (1, 1, 0),
    (-1, -1, 0),
    (1, -1, 0),
    (-1, 1, 0),
    (1, 0, 1),
    (-1, 0, -1),
    (1, 0, -1),
    (-1, 0, 1),
    (0, 1, 1),
    (0, -1, -1),
    (0, 1, -1),
    (0, -1, 1),
)
OPPOSITE = (0, 2, 1, 4, 3, 6, 5, 8, 7, 10, 9, 12, 11, 14, 13, 16, 15, 18, 17)
WEIGHTS = (1.0 / 3.0,) + (1.0 / 18.0,) * 6 + (1.0 / 36.0,) * 12
OMEGA = 1.25

EAST = tuple(d for d in range(19) if VELOCITIES[d][0] == 1)
WEST = tuple(d for d in range(19) if VELOCITIES[d][0] == -1)
NORTH = tuple(d for d in range(19) if VELOCITIES[d][1] == 1)
SOUTH = tuple(d for d in range(19) if VELOCITIES[d][1] == -1)
XDIRS = {1: EAST, -1: WEST}
YDIRS = {1: NORTH, -1: SOUTH}
CORNERS = ((1, 1), (-1, -1), (1, -1), (-1, 1))
CORNER_DIR = {(1, 1): 7, (-1, -1): 8, (1, -1): 9, (-1, 1): 10}

NEIGHBOURS = ((1, 0), (-1, 0), (0, 1), (0, -1)) + CORNERS
GROUPS = 4

CX, CY, NZ = 4, 8, 128
COLS = CX * CY


def dot_product(direction, vector):
    total = None
    for component in range(3):
        factor = VELOCITIES[direction][component]
        if factor != 0:
            term = vector[component] if factor == 1 else -vector[component]
            total = term if total is None else total + term
    return total


def moments(f):
    density = f[0]
    for d in range(1, 19):
        density = density + f[d]
    parts = []
    for component in range(3):
        plus = minus = None
        for d in range(19):
            factor = VELOCITIES[d][component]
            if factor == 1:
                plus = f[d] if plus is None else plus + f[d]
            elif factor == -1:
                minus = f[d] if minus is None else minus + f[d]
        parts.append(plus - minus)
    inverse = 1.0 / density
    return density, inverse, [part * inverse for part in parts]


def collide(f, density, inverse, velocity, field):
    half = 0.5 * inverse
    shifted = [velocity[c] + field[c] * half for c in range(3)]
    squared = shifted[0] * shifted[0] + shifted[1] * shifted[1] + shifted[2] * shifted[2]
    power = shifted[0] * field[0] + shifted[1] * field[1] + shifted[2] * field[2]
    gain = 1.0 - 0.5 * OMEGA
    scaled = OMEGA * density
    base = scaled * (1.0 - 1.5 * squared) - (3.0 * gain) * power
    curved = 4.5 * scaled
    sloped = 3.0 * scaled
    post = [None] * 19
    post[0] = (1.0 - OMEGA) * f[0] + WEIGHTS[0] * base
    for d in range(1, 19, 2):
        s = dot_product(d, shifted)
        g = dot_product(d, field)
        even = base + s * (curved * s + (9.0 * gain) * g)
        odd = sloped * s + (3.0 * gain) * g
        post[d] = (1.0 - OMEGA) * f[d] + WEIGHTS[d] * (even + odd)
        post[d + 1] = (1.0 - OMEGA) * f[d + 1] + WEIGHTS[d] * (even - odd)
    return post


def offsets(count):
    order = [0]
    for step in range(1, count // 2 + 1):
        order.append(step)
        if 2 * step != count:
            order.append(-step)
    return order


def kernel(
    n_gx,
    n_gy,
    pop_hbm,
    flags_hbm,
    tile_hbm,
    cell_hbm,
    frac_hbm,
    live_hbm,
    target_hbm,
    force_hbm,
    pop_out,
    force_out,
    state,
    post,
    moment_v,
    flags_v,
    tile_s,
    cell_v,
    frac_v,
    live_v,
    target_v,
    force_v,
    push_v,
    pull_v,
    send_a,
    recv_a,
    send_b,
    recv_b,
    send_c,
    recv_c,
    send_r,
    recv_r,
    force_now,
    sample_v,
    z_table,
    zt_table,
    c_table,
    s_table,
    v_table,
    solid_v,
    solid_row,
    back_row,
    flag_send,
    flag_recv,
    face_send,
    face_recv,
    edge_send,
    edge_recv,
    corner_send,
    corner_recv,
    in_sem,
    a_send_sem,
    a_recv_sem,
    b_send_sem,
    b_recv_sem,
    c_send_sem,
    c_recv_sem,
    r_send_sem,
    r_recv_sem,
    f_send_sem,
    f_recv_sem,
    h_send_sem,
    h_recv_sem,
):
    gx = lax.axis_index("gx")
    gy = lax.axis_index("gy")
    blocks = cell_v.shape[0]
    near = offsets(n_gx)
    place_of = {off % n_gx: n for n, off in enumerate(near)}
    far_first = list(range(n_gx - 1, 0, -1))

    def around(position, shift, count):
        return lax.rem(position + (shift + count), count)

    def device(dx, dy):
        if dy == 0:
            return {"gx": around(gx, dx, n_gx)}
        if dx == 0:
            return {"gy": around(gy, dy, n_gy)}
        return {"gx": around(gx, dx, n_gx), "gy": around(gy, dy, n_gy)}

    barrier = pltpu.get_barrier_semaphore()
    for n in far_first:
        pl.semaphore_signal(barrier, inc=1, device_id=device(near[n], 0), device_id_type=MESH)
    for dx, dy in NEIGHBOURS:
        if dy != 0:
            pl.semaphore_signal(barrier, inc=1, device_id=device(dx, dy), device_id_type=MESH)

    in_pairs = (
        (tile_hbm, tile_s),
        (cell_hbm, cell_v),
        (frac_hbm, frac_v),
        (live_hbm, live_v),
        (target_hbm, target_v),
        (force_hbm, force_v),
        (pop_hbm, state),
        (flags_hbm, flags_v),
    )
    loads = [
        pltpu.make_async_copy(src, dst, in_sem.at[i]) for i, (src, dst) in enumerate(in_pairs)
    ]
    for load in loads:
        load.start()
    for load in loads[:6]:
        load.wait()

    alive = live_v[...].astype(jnp.float32)
    for c in range(3):
        pull_v[c] = alive * target_v[c]
        push_v[c] = alive * (force_v[c] + target_v[c])

    def pack(t, carry):
        first = jnp.int32(-1)
        second = jnp.int32(-1)
        for b in range(blocks - 1, -1, -1):
            match = tile_s[0, b] == t
            second = jnp.where(match, first, second)
            first = jnp.where(match, jnp.int32(b), first)
        for s, index in enumerate((first, second)):
            valid = jnp.where(index >= 0, 1.0, 0.0)
            at = pl.ds(jnp.maximum(index, 0), 1)
            send_a[t, 4 * s : 4 * s + 1, :] = cell_v[at, :].astype(jnp.float32)
            for c in range(3):
                send_a[t, 4 * s + 1 + c : 4 * s + 2 + c, :] = frac_v[c, at, :]
                send_b[t, 4 * s + c : 4 * s + c + 1, :] = push_v[c, at, :] * valid
                send_c[t, 3 * s + c : 3 * s + c + 1, :] = pull_v[c, at, :] * valid
            send_b[t, 4 * s + 3 : 4 * s + 4, :] = live_v[at, :].astype(jnp.float32) * valid
        return carry

    lax.fori_loop(0, n_gx, pack, 0)
    recv_a[0] = send_a[gx]
    recv_b[0] = send_b[gx]
    recv_c[0] = send_c[gx]

    loads[7].wait()
    for number, (dx, dy) in enumerate(NEIGHBOURS):
        x = CX - 1 if dx == 1 else 0
        y = CY - 1 if dy == 1 else 0
        if dy == 0:
            flag_send[number] = flags_v[x].astype(jnp.float32)
        elif dx == 0:
            for x in range(CX):
                flag_send[number, x : x + 1, :] = flags_v[x, y : y + 1, :].astype(jnp.float32)
        else:
            flag_send[number, 0:1, :] = flags_v[x, y : y + 1, :].astype(jnp.float32)

    def peer_copy(send, recv, send_sem, recv_sem, rows=8):
        def copy(n):
            back = place_of[-near[n] % n_gx]
            return pltpu.make_async_remote_copy(
                src_ref=send.at[around(gx, near[n], n_gx), 0:rows],
                dst_ref=recv.at[back, 0:rows],
                send_sem=send_sem.at[n],
                recv_sem=recv_sem.at[back],
                device_id=device(near[n], 0),
                device_id_type=MESH,
            )

        return {n: copy(n) for n in far_first}

    def opposite(n):
        return place_of[-near[n] % n_gx]

    copies_a = peer_copy(send_a, recv_a, a_send_sem, a_recv_sem)
    copies_b = peer_copy(send_b, recv_b, b_send_sem, b_recv_sem)
    copies_c = peer_copy(send_c, recv_c, c_send_sem, c_recv_sem, 6)
    copies_r = {
        n: pltpu.make_async_remote_copy(
            src_ref=send_r.at[n, 0:6],
            dst_ref=recv_r.at[gx, 0:6],
            send_sem=r_send_sem.at[n],
            recv_sem=r_recv_sem.at[opposite(n)],
            device_id=device(near[n], 0),
            device_id_type=MESH,
        )
        for n in far_first
    }
    flag_rows = (CY, CY, CX, CX, 1, 1, 1, 1)
    copies_f = [
        pltpu.make_async_remote_copy(
            src_ref=flag_send.at[number, 0 : flag_rows[number]],
            dst_ref=flag_recv.at[number, 0 : flag_rows[number]],
            send_sem=f_send_sem.at[number],
            recv_sem=f_recv_sem.at[number],
            device_id=device(dx, dy),
            device_id_type=MESH,
        )
        for number, (dx, dy) in enumerate(NEIGHBOURS)
    ]

    pl.semaphore_wait(barrier, n_gx - 1 + 6)
    for n in far_first:
        copies_a[n].start()
    for n in far_first:
        copies_b[n].start()
    for copy in copies_f:
        copy.start()

    loads[6].wait()

    def velocity_tables(f):
        density, inverse, velocity = moments(f)
        moment_v[0] = density
        moment_v[1] = inverse
        for c in range(3):
            moment_v[2 + c] = velocity[c]
            rows = velocity[c].reshape(COLS, NZ)
            high = rows.astype(jnp.bfloat16)
            low = (rows - high.astype(jnp.float32)).astype(jnp.bfloat16)
            for half in range(2):
                v_table[c * COLS : (c + 1) * COLS, half * NZ : (half + 1) * NZ] = high
                v_table[(3 + c) * COLS : (4 + c) * COLS, half * NZ : (half + 1) * NZ] = low

    velocity_tables([state[d] for d in range(19)])

    y_rows = lax.broadcasted_iota(jnp.int32, (CY, NZ), 0)
    z_rows = lax.broadcasted_iota(jnp.int32, (16, NZ), 0)

    def build(n):
        for s in range(SLOT):
            begin = (n * SLOT + s) * NZ
            column = slice(begin, begin + NZ)
            cell = recv_a[n, 4 * s : 4 * s + 1, :].astype(jnp.int32)
            px = recv_a[n, 4 * s + 1 : 4 * s + 2, :]
            py = recv_a[n, 4 * s + 2 : 4 * s + 3, :]
            pz = recv_a[n, 4 * s + 3 : 4 * s + 4, :]
            i = lax.shift_right_logical(cell, 10)
            j = lax.shift_right_logical(cell, 7) & 7
            k = cell & 127
            wide = (CY, NZ)
            jw = jnp.broadcast_to(j, wide)
            pyw = jnp.broadcast_to(py, wide)
            wy = jnp.where(y_rows == jw, 1.0 - pyw, jnp.where(y_rows == jw + 1, pyw, 0.0))
            for x in range(CX):
                wx = jnp.where(i == x, 1.0 - px, jnp.where(i == x - 1, px, 0.0))
                c_table[x * CY : (x + 1) * CY, column] = jnp.broadcast_to(wx, wide) * wy
            tall = (16, NZ)
            kw = jnp.broadcast_to(k, tall)
            upper = jnp.broadcast_to(pz, tall)
            lower = 1.0 - upper
            upper_high = upper.astype(jnp.bfloat16)
            lower_high = lower.astype(jnp.bfloat16)
            upper_low = (upper - upper_high.astype(jnp.float32)).astype(jnp.bfloat16)
            lower_low = (lower - lower_high.astype(jnp.float32)).astype(jnp.bfloat16)
            k16 = kw.astype(jnp.bfloat16)
            none = jnp.zeros(tall, jnp.bfloat16)
            for chunk in range(NZ // 16):
                here = (z_rows + 16 * chunk).astype(jnp.bfloat16)
                below = (z_rows + (16 * chunk - 1)).astype(jnp.bfloat16)
                is_low = here == k16
                is_up = below == k16
                z_table[16 * chunk : 16 * chunk + 16, column] = jnp.where(
                    is_low, lower_high, jnp.where(is_up, upper_high, none)
                )
                z_table[NZ + 16 * chunk : NZ + 16 * chunk + 16, column] = jnp.where(
                    is_low, lower_low, jnp.where(is_up, upper_low, none)
                )

    def sample(n):
        wide = slice(n * SLOT * NZ, (n + 1) * SLOT * NZ)
        picked = jnp.dot(v_table[...], z_table[:, wide], preferred_element_type=jnp.float32)
        weights = c_table[:, wide]
        for c in range(3):
            both = (
                picked[c * COLS : (c + 1) * COLS] + picked[(3 + c) * COLS : (4 + c) * COLS]
            ) * weights
            sampled = jnp.sum(both, axis=0, keepdims=True)
            for s in range(SLOT):
                sample_v[n, 3 * s + c : 3 * s + c + 1, :] = sampled[:, s * NZ : (s + 1) * NZ]

    def push(n, step):
        for s in range(SLOT):
            rows = slice(3 * s, 3 * s + 3)
            column = slice((n * SLOT + s) * NZ, (n * SLOT + s + 1) * NZ)
            live = recv_b[n, 4 * s + 3 : 4 * s + 4, :]
            if step == 0:
                before = recv_b[n, 4 * s : 4 * s + 3, :]
            else:
                before = force_now[n, rows, :] + recv_c[n, rows, :]
            pushed = before - live * sample_v[n, rows, :]
            into = send_r if step == STEPS - 1 else force_now
            into[n, rows, :] = pushed
            for c in range(3):
                spread_row = c_table[:, column] * pushed[c : c + 1]
                high = spread_row.astype(jnp.bfloat16)
                low = (spread_row - high.astype(jnp.float32)).astype(jnp.bfloat16)
                s_table[c * COLS : (c + 1) * COLS, column] = high
                s_table[(3 + c) * COLS : (4 + c) * COLS, column] = low

    def spread(members, step):
        wide = slice(members[0] * SLOT * NZ, (members[-1] + 1) * SLOT * NZ)
        if step > 0:
            return jnp.dot(
                s_table[:, wide], zt_table[wide, :], preferred_element_type=jnp.float32
            )
        return lax.dot_general(
            s_table[:, wide],
            z_table[:, wide],
            (((1,), (1,)), ((), ())),
            preferred_element_type=jnp.float32,
        )

    def turn_table():
        for block in range(n_gx * SLOT):
            for half in range(2):
                zt_table[block * NZ : (block + 1) * NZ, half * NZ : (half + 1) * NZ] = z_table[
                    half * NZ : (half + 1) * NZ, block * NZ : (block + 1) * NZ
                ].T

    def rim_copies(step):
        def copy(number, src, dst):
            return pltpu.make_async_remote_copy(
                src_ref=src,
                dst_ref=dst,
                send_sem=h_send_sem.at[step, number],
                recv_sem=h_recv_sem.at[step, number],
                device_id=device(*NEIGHBOURS[number]),
                device_id_type=MESH,
            )

        out = []
        for number in range(8):
            if number < 2:
                out.append(
                    copy(number, face_send.at[step, number], face_recv.at[step, number])
                )
            elif number < 4:
                out.append(
                    copy(
                        number,
                        edge_send.at[step, number - 2, 0:20],
                        edge_recv.at[step, number - 2, 0:20],
                    )
                )
            else:
                out.append(
                    copy(
                        number,
                        corner_send.at[step, number - 4, 0:1],
                        corner_recv.at[step, number - 4, 0:1],
                    )
                )
        return out

    def shifted(tile, dy, dz):
        if dy != 0:
            tile = pltpu.roll(tile, 1 if dy == 1 else CY - 1, 0)
        if dz != 0:
            tile = pltpu.roll(tile, 1 if dz == 1 else NZ - 1, 1)
        return tile

    def solid_masks():
        tiles = [flags_v[x].astype(jnp.float32) for x in range(CX)]
        sublane = lax.broadcasted_iota(jnp.int32, (CY, NZ), 0)
        for d in range(1, 19):
            dx, dy, dz = VELOCITIES[d]
            for x in range(CX):
                from_x = x - dx
                outside = from_x < 0 or from_x >= CX
                if outside:
                    tile = flag_recv[NEIGHBOURS.index((dx, 0))]
                else:
                    tile = tiles[from_x]
                if dy != 0:
                    if outside:
                        row = flag_recv[NEIGHBOURS.index((dx, dy)), 0:1, :]
                    else:
                        row = flag_recv[NEIGHBOURS.index((0, dy)), from_x : from_x + 1, :]
                    edge = 0 if dy == 1 else CY - 1
                    tile = jnp.where(
                        sublane == edge, jnp.broadcast_to(row, (CY, NZ)), shifted(tile, dy, 0)
                    )
                solid_v[d, x] = shifted(tile, 0, dz)
        for side, sy in enumerate((1, -1)):
            y = 0 if sy == 1 else CY - 1
            solid_row[side] = jnp.zeros((24, NZ), jnp.float32)
            back_row[side] = jnp.zeros((24, NZ), jnp.float32)
            for place, d in enumerate(YDIRS[sy]):
                for from_x in range(CX):
                    x = from_x + VELOCITIES[d][0]
                    if 0 <= x < CX:
                        row = 4 * place + from_x
                        solid_row[side, row : row + 1, :] = solid_v[d, x, y : y + 1, :]

    def stream_inside(into):
        into[0] = post[0]
        for d in range(1, 19):
            dx, dy, dz = VELOCITIES[d]
            for x in range(CX):
                if 0 <= x - dx < CX:
                    moved = shifted(post[d, x - dx], dy, dz)
                    into[d, x] = jnp.where(solid_v[d, x] == 1.0, post[OPPOSITE[d], x], moved)
        for side, sy in enumerate((1, -1)):
            y = 0 if sy == 1 else CY - 1
            for place, d in enumerate(YDIRS[sy]):
                for from_x in range(CX):
                    x = from_x + VELOCITIES[d][0]
                    if 0 <= x < CX:
                        row = 4 * place + from_x
                        back_row[side, row : row + 1, :] = post[OPPOSITE[d], x, y : y + 1, :]

    def stream_edge(into, step, side):
        sy = (1, -1)[side]
        y = 0 if sy == 1 else CY - 1
        dirs = YDIRS[sy]
        half = lax.broadcasted_iota(jnp.int32, (8, NZ), 0) < 4
        parts = [edge_recv[step, side, 8 * p : 8 * p + (4 if p == 2 else 8), :] for p in range(3)]
        parts[1] = jnp.where(half, parts[1], shifted(parts[1], 0, VELOCITIES[dirs[3]][2]))
        parts[2] = shifted(parts[2], 0, VELOCITIES[dirs[4]][2])
        parts = [
            jnp.where(
                solid_row[side, 8 * p : 8 * p + parts[p].shape[0], :] == 1.0,
                back_row[side, 8 * p : 8 * p + parts[p].shape[0], :],
                parts[p],
            )
            for p in range(3)
        ]
        for place, d in enumerate(dirs):
            for from_x in range(CX):
                x = from_x + VELOCITIES[d][0]
                if 0 <= x < CX:
                    row = 4 * place + from_x
                    into[d, x, y : y + 1, :] = parts[row // 8][row % 8 : row % 8 + 1, :]

    def stream_face(into, step, side):
        sx = (1, -1)[side]
        x = 0 if sx == 1 else CX - 1
        for place, d in enumerate(XDIRS[sx]):
            _, dy, dz = VELOCITIES[d]
            moved = shifted(face_recv[step, side, place], dy, dz)
            into[d, x] = jnp.where(solid_v[d, x] == 1.0, post[OPPOSITE[d], x], moved)

    def stream_corner(into, step, corner):
        sx, sy = CORNERS[corner]
        d = CORNER_DIR[sx, sy]
        x = 0 if sx == 1 else CX - 1
        y = slice(0, 1) if sy == 1 else slice(CY - 1, CY)
        into[d, x, y, :] = jnp.where(
            solid_v[d, x, y, :] == 1.0,
            post[OPPOSITE[d], x, y, :],
            corner_recv[step, corner, 0:1, :],
        )

    per = n_gx // GROUPS
    groups = [list(range(g * per, (g + 1) * per)) for g in range(GROUPS)]
    rims = None
    for step in range(STEPS):
        last = step == STEPS - 1
        total = None
        if step == 0:
            for members in groups:
                for n in members:
                    if n > 0:
                        copies_a[opposite(n)].wait_recv()
                for n in members:
                    build(n)
                for n in members:
                    sample(n)
        for members in groups:
            if step == 0:
                for n in members:
                    if n > 0:
                        copies_b[opposite(n)].wait_recv()
            else:
                for n in members:
                    sample(n)
                if members is groups[0]:
                    for n in far_first:
                        copies_c[opposite(n)].wait_recv()
            for n in members:
                push(n, step)
            if step == 0 and members is groups[0]:
                for n in far_first:
                    copies_c[n].start()
            part = spread(members, step)
            total = part if total is None else total + part
        field = (total[: 3 * COLS, :NZ] + total[3 * COLS :, :NZ]) + (
            total[: 3 * COLS, NZ:] + total[3 * COLS :, NZ:]
        )
        field = field.reshape(3, CX, CY, NZ)
        f = [state[d] for d in range(19)]
        after = collide(
            f,
            moment_v[0],
            moment_v[1],
            [moment_v[2 + c] for c in range(3)],
            [field[c] for c in range(3)],
        )
        copies = rim_copies(step)
        for corner, (sx, sy) in enumerate(CORNERS):
            x = CX - 1 if sx == 1 else 0
            y = CY - 1 if sy == 1 else 0
            corner_send[step, corner, 0:1, :] = after[CORNER_DIR[sx, sy]][x, y : y + 1, :]
        for side, sx in enumerate((1, -1)):
            for place, d in enumerate(XDIRS[sx]):
                face_send[step, side, place] = after[d][CX - 1 if sx == 1 else 0]
        for side, sy in enumerate((1, -1)):
            y = CY - 1 if sy == 1 else 0
            for place, d in enumerate(YDIRS[sy]):
                for x in range(CX):
                    row = 4 * place + x
                    edge_send[step, side, row : row + 1, :] = after[d][x, y : y + 1, :]
        for number in (4, 5, 6, 7, 0, 1, 2, 3):
            copies[number].start()
        if last:
            recv_r[gx] = send_r[0]
            for n in far_first:
                copies_r[n].start()
        for d in range(19):
            post[d] = after[d]
        into = pop_out if last else state
        if last:
            homes = [tile_s[0, b] for b in range(blocks)]
            starts = []
            for b in range(blocks):
                rank = jnp.int32(0)
                for other in range(b):
                    rank = rank + jnp.where(homes[other] == homes[b], 3, 0)
                starts.append(jnp.minimum(rank, 3))
        if step == 0:
            for copy in copies_f:
                copy.wait_recv()
            turn_table()
            solid_masks()
        stream_inside(into)
        if last:
            for kind in (copies_a, copies_b, copies_c):
                for n in far_first:
                    kind[n].wait_send()
            for copy in copies_f + rims:
                copy.wait_send()
        rims = copies
        for side in range(2):
            copies[2 + side].wait_recv()
            stream_edge(into, step, side)
        for side in range(2):
            copies[side].wait_recv()
            stream_face(into, step, side)
        for corner in range(4):
            copies[4 + corner].wait_recv()
            stream_corner(into, step, corner)
        if last:
            for n in far_first:
                copies_r[opposite(n)].wait_recv()
            for b in range(blocks):
                half = recv_r[homes[b], pl.ds(starts[b], 3), :]
                for c in range(3):
                    push_v[c, b : b + 1, :] = half[c : c + 1]
            keep = live_v[...] == 1
            for c in range(3):
                force_out[c] = jnp.where(keep, push_v[c], force_v[c])
        if not last:
            velocity_tables([state[d] for d in range(19)])

    for n in far_first:
        copies_r[n].wait_send()
    for copy in copies:
        copy.wait_send()


def deliver(state, force, state_out, force_out, sem):
    copies = [
        pltpu.make_async_copy(state, state_out, sem.at[0]),
        pltpu.make_async_copy(force, force_out, sem.at[1]),
    ]
    for copy in copies:
        copy.start()
    for copy in copies:
        copy.wait()


def body(
    populations,
    flags,
    block_tile,
    marker_cell,
    marker_frac,
    marker_live,
    marker_target,
    marker_force,
):
    n_gx = lax.axis_size("gx")
    n_gy = lax.axis_size("gy")
    blocks, markers = marker_cell.shape
    width = n_gx * SLOT * markers
    marker_rows = (3, blocks, markers)
    packed = (n_gx, 8, markers)
    f32, bf16, i32 = jnp.float32, jnp.bfloat16, jnp.int32
    dma = pltpu.SemaphoreType.DMA
    vmem = pltpu.VMEM
    in_hbm = functools.partial(pltpu.with_memory_space_constraint, memory_space=pltpu.HBM)
    in_vmem = functools.partial(pltpu.with_memory_space_constraint, memory_space=pltpu.VMEM)
    anywhere = pl.BlockSpec(memory_space=pl.ANY)
    inside = pl.BlockSpec(memory_space=pltpu.VMEM)
    state, force = pl.pallas_call(
        functools.partial(kernel, n_gx, n_gy),
        out_shape=(vmem(populations.shape, f32), vmem(marker_rows, f32)),
        in_specs=[anywhere] * 8,
        out_specs=(inside, inside),
        scratch_shapes=[
            vmem(populations.shape, f32),
            vmem(populations.shape, f32),
            vmem((5, CX, CY, NZ), f32),
            vmem(flags.shape, i32),
            pltpu.SMEM((1, blocks), i32),
            vmem(marker_cell.shape, i32),
            vmem(marker_rows, f32),
            vmem(marker_live.shape, i32),
            vmem(marker_rows, f32),
            vmem(marker_rows, f32),
            vmem(marker_rows, f32),
            vmem(marker_rows, f32),
        ]
        + [vmem(packed, f32)] * 10
        + [
            vmem((2 * NZ, width), bf16),
            vmem((width, 2 * NZ), bf16),
            vmem((COLS, width), f32),
            vmem((6 * COLS, width), bf16),
            vmem((6 * COLS, 2 * NZ), bf16),
            vmem(populations.shape, f32),
            vmem((2, 24, NZ), f32),
            vmem((2, 24, NZ), f32),
            vmem((8, CY, NZ), f32),
            vmem((8, CY, NZ), f32),
            vmem((STEPS, 2, 5, CY, NZ), f32),
            vmem((STEPS, 2, 5, CY, NZ), f32),
            vmem((STEPS, 2, 24, NZ), f32),
            vmem((STEPS, 2, 24, NZ), f32),
            vmem((STEPS, 4, 8, NZ), f32),
            vmem((STEPS, 4, 8, NZ), f32),
            dma((8,)),
        ]
        + [dma((n_gx,))] * 8
        + [dma((8,))] * 2
        + [dma((STEPS, 8))] * 2,
        compiler_params=pltpu.CompilerParams(
            collective_id=0,
            has_side_effects=True,
            vmem_limit_bytes=32 * 1024 * 1024,
        ),
    )(
        in_hbm(populations),
        in_hbm(flags),
        in_hbm(block_tile.T),
        in_hbm(marker_cell),
        in_hbm(marker_frac.transpose(1, 0, 2)),
        in_hbm(marker_live),
        in_hbm(marker_target.transpose(1, 0, 2)),
        in_hbm(marker_force.transpose(1, 0, 2)),
    )
    state, force = pl.pallas_call(
        deliver,
        out_shape=(
            jax.ShapeDtypeStruct(populations.shape, f32),
            jax.ShapeDtypeStruct(marker_rows, f32),
        ),
        in_specs=[inside] * 2,
        out_specs=(anywhere, anywhere),
        scratch_shapes=[dma((2,))],
    )(in_vmem(state), in_vmem(force))
    return state, force.transpose(1, 0, 2)


def solution(mesh):
    in_specs = (
        P(None, "gx", "gy", None),
        P("gx", "gy", None),
        P(("gx", "gy"), None),
        P(("gx", "gy"), None),
        P(("gx", "gy"), None, None),
        P(("gx", "gy"), None),
        P(("gx", "gy"), None, None),
        P(("gx", "gy"), None, None),
    )
    out_specs = (P(None, "gx", "gy", None), P(("gx", "gy"), None, None))
    return jax.shard_map(body, mesh=mesh, in_specs=in_specs, out_specs=out_specs, check_vma=False)
```

```python
import functools

import jax
import jax.numpy as jnp
from jax import lax
from jax.experimental import pallas as pl
from jax.experimental.pallas import tpu as pltpu
from jax.sharding import PartitionSpec as P

STEPS = 2
SLOT = 2
MESH = pl.DeviceIdType.MESH

VELOCITIES = (
    (0, 0, 0),
    (1, 0, 0),
    (-1, 0, 0),
    (0, 1, 0),
    (0, -1, 0),
    (0, 0, 1),
    (0, 0, -1),
    (1, 1, 0),
    (-1, -1, 0),
    (1, -1, 0),
    (-1, 1, 0),
    (1, 0, 1),
    (-1, 0, -1),
    (1, 0, -1),
    (-1, 0, 1),
    (0, 1, 1),
    (0, -1, -1),
    (0, 1, -1),
    (0, -1, 1),
)
OPPOSITE = (0, 2, 1, 4, 3, 6, 5, 8, 7, 10, 9, 12, 11, 14, 13, 16, 15, 18, 17)
WEIGHTS = (1.0 / 3.0,) + (1.0 / 18.0,) * 6 + (1.0 / 36.0,) * 12
OMEGA = 1.25

EAST = tuple(d for d in range(19) if VELOCITIES[d][0] == 1)
WEST = tuple(d for d in range(19) if VELOCITIES[d][0] == -1)
NORTH = tuple(d for d in range(19) if VELOCITIES[d][1] == 1)
SOUTH = tuple(d for d in range(19) if VELOCITIES[d][1] == -1)
XDIRS = {1: EAST, -1: WEST}
YDIRS = {1: NORTH, -1: SOUTH}
CORNERS = ((1, 1), (-1, -1), (1, -1), (-1, 1))
CORNER_DIR = {(1, 1): 7, (-1, -1): 8, (1, -1): 9, (-1, 1): 10}

NEIGHBOURS = ((1, 0), (-1, 0), (0, 1), (0, -1)) + CORNERS
GROUPS = 4

CX, CY, NZ = 4, 8, 128
COLS = CX * CY


def dot_product(direction, vector):
    total = None
    for component in range(3):
        factor = VELOCITIES[direction][component]
        if factor != 0:
            term = vector[component] if factor == 1 else -vector[component]
            total = term if total is None else total + term
    return total


def moments(f):
    density = f[0]
    for d in range(1, 19):
        density = density + f[d]
    parts = []
    for component in range(3):
        plus = minus = None
        for d in range(19):
            factor = VELOCITIES[d][component]
            if factor == 1:
                plus = f[d] if plus is None else plus + f[d]
            elif factor == -1:
                minus = f[d] if minus is None else minus + f[d]
        parts.append(plus - minus)
    inverse = 1.0 / density
    return density, inverse, [part * inverse for part in parts]


def collide(f, density, inverse, velocity, field):
    half = 0.5 * inverse
    shifted = [velocity[c] + field[c] * half for c in range(3)]
    squared = shifted[0] * shifted[0] + shifted[1] * shifted[1] + shifted[2] * shifted[2]
    power = shifted[0] * field[0] + shifted[1] * field[1] + shifted[2] * field[2]
    gain = 1.0 - 0.5 * OMEGA
    scaled = OMEGA * density
    base = scaled * (1.0 - 1.5 * squared) - (3.0 * gain) * power
    curved = 4.5 * scaled
    sloped = 3.0 * scaled
    post = [None] * 19
    post[0] = (1.0 - OMEGA) * f[0] + WEIGHTS[0] * base
    for d in range(1, 19, 2):
        s = dot_product(d, shifted)
        g = dot_product(d, field)
        even = base + s * (curved * s + (9.0 * gain) * g)
        odd = sloped * s + (3.0 * gain) * g
        post[d] = (1.0 - OMEGA) * f[d] + WEIGHTS[d] * (even + odd)
        post[d + 1] = (1.0 - OMEGA) * f[d + 1] + WEIGHTS[d] * (even - odd)
    return post


def offsets(count):
    order = [0]
    for step in range(1, count // 2 + 1):
        order.append(step)
        if 2 * step != count:
            order.append(-step)
    return order


def kernel(
    n_gx,
    n_gy,
    pop_hbm,
    flags_hbm,
    tile_hbm,
    cell_hbm,
    frac_hbm,
    live_hbm,
    target_hbm,
    force_hbm,
    pop_out,
    force_out,
    state,
    post,
    moment_v,
    flags_v,
    tile_s,
    cell_v,
    frac_v,
    live_v,
    target_v,
    force_v,
    push_v,
    pull_v,
    send_a,
    recv_a,
    send_b,
    recv_b,
    send_c,
    recv_c,
    send_r,
    recv_r,
    force_now,
    sample_v,
    z_table,
    zt_table,
    c_table,
    s_table,
    v_table,
    solid_v,
    solid_row,
    back_row,
    flag_send,
    flag_recv,
    face_send,
    face_recv,
    edge_send,
    edge_recv,
    corner_send,
    corner_recv,
    in_sem,
    a_send_sem,
    a_recv_sem,
    b_send_sem,
    b_recv_sem,
    c_send_sem,
    c_recv_sem,
    r_send_sem,
    r_recv_sem,
    f_send_sem,
    f_recv_sem,
    h_send_sem,
    h_recv_sem,
):
    gx = lax.axis_index("gx")
    gy = lax.axis_index("gy")
    blocks = cell_v.shape[0]
    near = offsets(n_gx)
    place_of = {off % n_gx: n for n, off in enumerate(near)}
    far_first = list(range(n_gx - 1, 0, -1))

    def around(position, shift, count):
        return lax.rem(position + (shift + count), count)

    def device(dx, dy):
        if dy == 0:
            return {"gx": around(gx, dx, n_gx)}
        if dx == 0:
            return {"gy": around(gy, dy, n_gy)}
        return {"gx": around(gx, dx, n_gx), "gy": around(gy, dy, n_gy)}

    barrier = pltpu.get_barrier_semaphore()
    for n in far_first:
        pl.semaphore_signal(barrier, inc=1, device_id=device(near[n], 0), device_id_type=MESH)
    for dx, dy in NEIGHBOURS:
        if dx == 0:
            pl.semaphore_signal(barrier, inc=1, device_id=device(dx, dy), device_id_type=MESH)

    in_pairs = (
        (tile_hbm, tile_s),
        (cell_hbm, cell_v),
        (frac_hbm, frac_v),
        (live_hbm, live_v),
        (target_hbm, target_v),
        (force_hbm, force_v),
        (pop_hbm, state),
        (flags_hbm, flags_v),
    )
    loads = [
        pltpu.make_async_copy(src, dst, in_sem.at[i]) for i, (src, dst) in enumerate(in_pairs)
    ]
    for load in loads:
        load.start()
    for load in loads[:6]:
        load.wait()

    alive = live_v[...].astype(jnp.float32)
    for c in range(3):
        pull_v[c] = alive * target_v[c]
        push_v[c] = alive * (force_v[c] + target_v[c])

    def pack(t, carry):
        first = jnp.int32(-1)
        second = jnp.int32(-1)
        for b in range(blocks - 1, -1, -1):
            match = tile_s[0, b] == t
            second = jnp.where(match, first, second)
            first = jnp.where(match, jnp.int32(b), first)
        for s, index in enumerate((first, second)):
            valid = jnp.where(index >= 0, 1.0, 0.0)
            at = pl.ds(jnp.maximum(index, 0), 1)
            send_a[t, 4 * s : 4 * s + 1, :] = cell_v[at, :].astype(jnp.float32)
            for c in range(3):
                send_a[t, 4 * s + 1 + c : 4 * s + 2 + c, :] = frac_v[c, at, :]
                send_b[t, 4 * s + c : 4 * s + c + 1, :] = push_v[c, at, :] * valid
                send_c[t, 3 * s + c : 3 * s + c + 1, :] = pull_v[c, at, :] * valid
            send_b[t, 4 * s + 3 : 4 * s + 4, :] = live_v[at, :].astype(jnp.float32) * valid
        return carry

    lax.fori_loop(0, n_gx, pack, 0)
    recv_a[0] = send_a[gx]
    recv_b[0] = send_b[gx]
    recv_c[0] = send_c[gx]

    loads[7].wait()
    for number, (dx, dy) in enumerate(NEIGHBOURS):
        x = CX - 1 if dx == 1 else 0
        y = CY - 1 if dy == 1 else 0
        if dy == 0:
            flag_send[number] = flags_v[x].astype(jnp.float32)
        elif dx == 0:
            for x in range(CX):
                flag_send[number, x : x + 1, :] = flags_v[x, y : y + 1, :].astype(jnp.float32)
        else:
            flag_send[number, 0:1, :] = flags_v[x, y : y + 1, :].astype(jnp.float32)

    def peer_copy(send, recv, send_sem, recv_sem, rows=8):
        def copy(n):
            back = place_of[-near[n] % n_gx]
            return pltpu.make_async_remote_copy(
                src_ref=send.at[around(gx, near[n], n_gx), 0:rows],
                dst_ref=recv.at[back, 0:rows],
                send_sem=send_sem.at[n],
                recv_sem=recv_sem.at[back],
                device_id=device(near[n], 0),
                device_id_type=MESH,
            )

        return {n: copy(n) for n in far_first}

    def opposite(n):
        return place_of[-near[n] % n_gx]

    copies_a = peer_copy(send_a, recv_a, a_send_sem, a_recv_sem)
    copies_b = peer_copy(send_b, recv_b, b_send_sem, b_recv_sem)
    copies_c = peer_copy(send_c, recv_c, c_send_sem, c_recv_sem, 6)
    copies_r = {
        n: pltpu.make_async_remote_copy(
            src_ref=send_r.at[n, 0:6],
            dst_ref=recv_r.at[gx, 0:6],
            send_sem=r_send_sem.at[n],
            recv_sem=r_recv_sem.at[opposite(n)],
            device_id=device(near[n], 0),
            device_id_type=MESH,
        )
        for n in far_first
    }
    flag_rows = (CY, CY, CX, CX, 1, 1, 1, 1)
    copies_f = [
        pltpu.make_async_remote_copy(
            src_ref=flag_send.at[number, 0 : flag_rows[number]],
            dst_ref=flag_recv.at[number, 0 : flag_rows[number]],
            send_sem=f_send_sem.at[number],
            recv_sem=f_recv_sem.at[number],
            device_id=device(dx, dy),
            device_id_type=MESH,
        )
        for number, (dx, dy) in enumerate(NEIGHBOURS)
    ]

    pl.semaphore_wait(barrier, n_gx - 1 + 2)
    for n in far_first:
        copies_a[n].start()
    for n in far_first:
        copies_b[n].start()

    loads[6].wait()

    def velocity_tables(f):
        density, inverse, velocity = moments(f)
        moment_v[0] = density
        moment_v[1] = inverse
        for c in range(3):
            moment_v[2 + c] = velocity[c]
            rows = velocity[c].reshape(COLS, NZ)
            high = rows.astype(jnp.bfloat16)
            low = (rows - high.astype(jnp.float32)).astype(jnp.bfloat16)
            for half in range(2):
                v_table[c * COLS : (c + 1) * COLS, half * NZ : (half + 1) * NZ] = high
                v_table[(3 + c) * COLS : (4 + c) * COLS, half * NZ : (half + 1) * NZ] = low

    velocity_tables([state[d] for d in range(19)])

    y_rows = lax.broadcasted_iota(jnp.int32, (CY, NZ), 0)
    z_rows = lax.broadcasted_iota(jnp.int32, (16, NZ), 0)

    def build(n):
        for s in range(SLOT):
            begin = (n * SLOT + s) * NZ
            column = slice(begin, begin + NZ)
            cell = recv_a[n, 4 * s : 4 * s + 1, :].astype(jnp.int32)
            px = recv_a[n, 4 * s + 1 : 4 * s + 2, :]
            py = recv_a[n, 4 * s + 2 : 4 * s + 3, :]
            pz = recv_a[n, 4 * s + 3 : 4 * s + 4, :]
            i = lax.shift_right_logical(cell, 10)
            j = lax.shift_right_logical(cell, 7) & 7
            k = cell & 127
            wide = (CY, NZ)
            jw = jnp.broadcast_to(j, wide)
            pyw = jnp.broadcast_to(py, wide)
            wy = jnp.where(y_rows == jw, 1.0 - pyw, jnp.where(y_rows == jw + 1, pyw, 0.0))
            for x in range(CX):
                wx = jnp.where(i == x, 1.0 - px, jnp.where(i == x - 1, px, 0.0))
                c_table[x * CY : (x + 1) * CY, column] = jnp.broadcast_to(wx, wide) * wy
            tall = (16, NZ)
            kw = jnp.broadcast_to(k, tall)
            upper = jnp.broadcast_to(pz, tall)
            lower = 1.0 - upper
            upper_high = upper.astype(jnp.bfloat16)
            lower_high = lower.astype(jnp.bfloat16)
            upper_low = (upper - upper_high.astype(jnp.float32)).astype(jnp.bfloat16)
            lower_low = (lower - lower_high.astype(jnp.float32)).astype(jnp.bfloat16)
            k16 = kw.astype(jnp.bfloat16)
            none = jnp.zeros(tall, jnp.bfloat16)
            for chunk in range(NZ // 16):
                here = (z_rows + 16 * chunk).astype(jnp.bfloat16)
                below = (z_rows + (16 * chunk - 1)).astype(jnp.bfloat16)
                is_low = here == k16
                is_up = below == k16
                z_table[16 * chunk : 16 * chunk + 16, column] = jnp.where(
                    is_low, lower_high, jnp.where(is_up, upper_high, none)
                )
                z_table[NZ + 16 * chunk : NZ + 16 * chunk + 16, column] = jnp.where(
                    is_low, lower_low, jnp.where(is_up, upper_low, none)
                )

    def sample(n):
        wide = slice(n * SLOT * NZ, (n + 1) * SLOT * NZ)
        picked = jnp.dot(v_table[...], z_table[:, wide], preferred_element_type=jnp.float32)
        weights = c_table[:, wide]
        for c in range(3):
            both = (
                picked[c * COLS : (c + 1) * COLS] + picked[(3 + c) * COLS : (4 + c) * COLS]
            ) * weights
            sampled = jnp.sum(both, axis=0, keepdims=True)
            for s in range(SLOT):
                sample_v[n, 3 * s + c : 3 * s + c + 1, :] = sampled[:, s * NZ : (s + 1) * NZ]

    def push(n, step):
        for s in range(SLOT):
            rows = slice(3 * s, 3 * s + 3)
            column = slice((n * SLOT + s) * NZ, (n * SLOT + s + 1) * NZ)
            live = recv_b[n, 4 * s + 3 : 4 * s + 4, :]
            if step == 0:
                before = recv_b[n, 4 * s : 4 * s + 3, :]
            else:
                before = force_now[n, rows, :] + recv_c[n, rows, :]
            pushed = before - live * sample_v[n, rows, :]
            into = send_r if step == STEPS - 1 else force_now
            into[n, rows, :] = pushed
            for c in range(3):
                spread_row = c_table[:, column] * pushed[c : c + 1]
                high = spread_row.astype(jnp.bfloat16)
                low = (spread_row - high.astype(jnp.float32)).astype(jnp.bfloat16)
                s_table[c * COLS : (c + 1) * COLS, column] = high
                s_table[(3 + c) * COLS : (4 + c) * COLS, column] = low

    def spread(members, step):
        wide = slice(members[0] * SLOT * NZ, (members[-1] + 1) * SLOT * NZ)
        if step > 0:
            return jnp.dot(
                s_table[:, wide], zt_table[wide, :], preferred_element_type=jnp.float32
            )
        return lax.dot_general(
            s_table[:, wide],
            z_table[:, wide],
            (((1,), (1,)), ((), ())),
            preferred_element_type=jnp.float32,
        )

    def turn_table():
        for block in range(n_gx * SLOT):
            for half in range(2):
                zt_table[block * NZ : (block + 1) * NZ, half * NZ : (half + 1) * NZ] = z_table[
                    half * NZ : (half + 1) * NZ, block * NZ : (block + 1) * NZ
                ].T

    def rim_copies(step):
        def copy(number, src, dst):
            return pltpu.make_async_remote_copy(
                src_ref=src,
                dst_ref=dst,
                send_sem=h_send_sem.at[step, number],
                recv_sem=h_recv_sem.at[step, number],
                device_id=device(*NEIGHBOURS[number]),
                device_id_type=MESH,
            )

        out = []
        for number in range(8):
            if number < 2:
                out.append(
                    copy(number, face_send.at[step, number], face_recv.at[step, number])
                )
            elif number < 4:
                out.append(
                    copy(
                        number,
                        edge_send.at[step, number - 2, 0:20],
                        edge_recv.at[step, number - 2, 0:20],
                    )
                )
            else:
                out.append(
                    copy(
                        number,
                        corner_send.at[step, number - 4, 0:1],
                        corner_recv.at[step, number - 4, 0:1],
                    )
                )
        return out

    def shifted(tile, dy, dz):
        if dy != 0:
            tile = pltpu.roll(tile, 1 if dy == 1 else CY - 1, 0)
        if dz != 0:
            tile = pltpu.roll(tile, 1 if dz == 1 else NZ - 1, 1)
        return tile

    def solid_masks():
        tiles = [flags_v[x].astype(jnp.float32) for x in range(CX)]
        sublane = lax.broadcasted_iota(jnp.int32, (CY, NZ), 0)
        for d in range(1, 19):
            dx, dy, dz = VELOCITIES[d]
            for x in range(CX):
                from_x = x - dx
                outside = from_x < 0 or from_x >= CX
                if outside:
                    tile = flag_recv[NEIGHBOURS.index((dx, 0))]
                else:
                    tile = tiles[from_x]
                if dy != 0:
                    if outside:
                        row = flag_recv[NEIGHBOURS.index((dx, dy)), 0:1, :]
                    else:
                        row = flag_recv[NEIGHBOURS.index((0, dy)), from_x : from_x + 1, :]
                    edge = 0 if dy == 1 else CY - 1
                    tile = jnp.where(
                        sublane == edge, jnp.broadcast_to(row, (CY, NZ)), shifted(tile, dy, 0)
                    )
                solid_v[d, x] = shifted(tile, 0, dz)
        for side, sy in enumerate((1, -1)):
            y = 0 if sy == 1 else CY - 1
            solid_row[side] = jnp.zeros((24, NZ), jnp.float32)
            back_row[side] = jnp.zeros((24, NZ), jnp.float32)
            for place, d in enumerate(YDIRS[sy]):
                for from_x in range(CX):
                    x = from_x + VELOCITIES[d][0]
                    if 0 <= x < CX:
                        row = 4 * place + from_x
                        solid_row[side, row : row + 1, :] = solid_v[d, x, y : y + 1, :]

    def stream_inside(into):
        into[0] = post[0]
        for d in range(1, 19):
            dx, dy, dz = VELOCITIES[d]
            for x in range(CX):
                if 0 <= x - dx < CX:
                    moved = shifted(post[d, x - dx], dy, dz)
                    into[d, x] = jnp.where(solid_v[d, x] == 1.0, post[OPPOSITE[d], x], moved)
        for side, sy in enumerate((1, -1)):
            y = 0 if sy == 1 else CY - 1
            for place, d in enumerate(YDIRS[sy]):
                for from_x in range(CX):
                    x = from_x + VELOCITIES[d][0]
                    if 0 <= x < CX:
                        row = 4 * place + from_x
                        back_row[side, row : row + 1, :] = post[OPPOSITE[d], x, y : y + 1, :]

    def stream_edge(into, step, side):
        sy = (1, -1)[side]
        y = 0 if sy == 1 else CY - 1
        dirs = YDIRS[sy]
        half = lax.broadcasted_iota(jnp.int32, (8, NZ), 0) < 4
        parts = [edge_recv[step, side, 8 * p : 8 * p + (4 if p == 2 else 8), :] for p in range(3)]
        parts[1] = jnp.where(half, parts[1], shifted(parts[1], 0, VELOCITIES[dirs[3]][2]))
        parts[2] = shifted(parts[2], 0, VELOCITIES[dirs[4]][2])
        parts = [
            jnp.where(
                solid_row[side, 8 * p : 8 * p + parts[p].shape[0], :] == 1.0,
                back_row[side, 8 * p : 8 * p + parts[p].shape[0], :],
                parts[p],
            )
            for p in range(3)
        ]
        for place, d in enumerate(dirs):
            for from_x in range(CX):
                x = from_x + VELOCITIES[d][0]
                if 0 <= x < CX:
                    row = 4 * place + from_x
                    into[d, x, y : y + 1, :] = parts[row // 8][row % 8 : row % 8 + 1, :]

    def stream_face(into, step, side):
        sx = (1, -1)[side]
        x = 0 if sx == 1 else CX - 1
        for place, d in enumerate(XDIRS[sx]):
            _, dy, dz = VELOCITIES[d]
            moved = shifted(face_recv[step, side, place], dy, dz)
            into[d, x] = jnp.where(solid_v[d, x] == 1.0, post[OPPOSITE[d], x], moved)

    def stream_corner(into, step, corner):
        sx, sy = CORNERS[corner]
        d = CORNER_DIR[sx, sy]
        x = 0 if sx == 1 else CX - 1
        y = slice(0, 1) if sy == 1 else slice(CY - 1, CY)
        into[d, x, y, :] = jnp.where(
            solid_v[d, x, y, :] == 1.0,
            post[OPPOSITE[d], x, y, :],
            corner_recv[step, corner, 0:1, :],
        )

    per = n_gx // GROUPS
    groups = [list(range(g * per, (g + 1) * per)) for g in range(GROUPS)]
    rims = None
    for step in range(STEPS):
        last = step == STEPS - 1
        total = None
        if step == 0:
            for members in groups:
                for n in members:
                    if n > 0:
                        copies_a[opposite(n)].wait_recv()
                for n in members:
                    build(n)
                for n in members:
                    sample(n)
        if step == 0:
            for copy in copies_f:
                copy.start()
        for members in groups:
            if step == 0:
                for n in members:
                    if n > 0:
                        copies_b[opposite(n)].wait_recv()
            else:
                for n in members:
                    sample(n)
                if members is groups[0]:
                    for n in far_first:
                        copies_c[opposite(n)].wait_recv()
            for n in members:
                push(n, step)
            if step == 0 and members is groups[0]:
                for n in far_first:
                    copies_c[n].start()
            part = spread(members, step)
            total = part if total is None else total + part
        field = (total[: 3 * COLS, :NZ] + total[3 * COLS :, :NZ]) + (
            total[: 3 * COLS, NZ:] + total[3 * COLS :, NZ:]
        )
        field = field.reshape(3, CX, CY, NZ)
        f = [state[d] for d in range(19)]
        after = collide(
            f,
            moment_v[0],
            moment_v[1],
            [moment_v[2 + c] for c in range(3)],
            [field[c] for c in range(3)],
        )
        copies = rim_copies(step)
        for corner, (sx, sy) in enumerate(CORNERS):
            x = CX - 1 if sx == 1 else 0
            y = CY - 1 if sy == 1 else 0
            corner_send[step, corner, 0:1, :] = after[CORNER_DIR[sx, sy]][x, y : y + 1, :]
        for side, sx in enumerate((1, -1)):
            for place, d in enumerate(XDIRS[sx]):
                face_send[step, side, place] = after[d][CX - 1 if sx == 1 else 0]
        for side, sy in enumerate((1, -1)):
            y = CY - 1 if sy == 1 else 0
            for place, d in enumerate(YDIRS[sy]):
                for x in range(CX):
                    row = 4 * place + x
                    edge_send[step, side, row : row + 1, :] = after[d][x, y : y + 1, :]
        for number in (4, 5, 6, 7, 0, 1, 2, 3):
            copies[number].start()
        if last:
            recv_r[gx] = send_r[0]
            for n in far_first:
                copies_r[n].start()
        for d in range(19):
            post[d] = after[d]
        into = pop_out if last else state
        if last:
            homes = [tile_s[0, b] for b in range(blocks)]
            starts = []
            for b in range(blocks):
                rank = jnp.int32(0)
                for other in range(b):
                    rank = rank + jnp.where(homes[other] == homes[b], 3, 0)
                starts.append(jnp.minimum(rank, 3))
        if step == 0:
            for copy in copies_f:
                copy.wait_recv()
            turn_table()
            solid_masks()
        stream_inside(into)
        if last:
            for kind in (copies_a, copies_b, copies_c):
                for n in far_first:
                    kind[n].wait_send()
            for copy in copies_f + rims:
                copy.wait_send()
        rims = copies
        for side in range(2):
            copies[2 + side].wait_recv()
            stream_edge(into, step, side)
        for side in range(2):
            copies[side].wait_recv()
            stream_face(into, step, side)
        for corner in range(4):
            copies[4 + corner].wait_recv()
            stream_corner(into, step, corner)
        if last:
            for n in far_first:
                copies_r[opposite(n)].wait_recv()
            for b in range(blocks):
                half = recv_r[homes[b], pl.ds(starts[b], 3), :]
                for c in range(3):
                    push_v[c, b : b + 1, :] = half[c : c + 1]
            keep = live_v[...] == 1
            for c in range(3):
                force_out[c] = jnp.where(keep, push_v[c], force_v[c])
        if not last:
            velocity_tables([state[d] for d in range(19)])

    for n in far_first:
        copies_r[n].wait_send()
    for copy in copies:
        copy.wait_send()


def deliver(state, force, state_out, force_out, sem):
    copies = [
        pltpu.make_async_copy(state, state_out, sem.at[0]),
        pltpu.make_async_copy(force, force_out, sem.at[1]),
    ]
    for copy in copies:
        copy.start()
    for copy in copies:
        copy.wait()


def body(
    populations,
    flags,
    block_tile,
    marker_cell,
    marker_frac,
    marker_live,
    marker_target,
    marker_force,
):
    n_gx = lax.axis_size("gx")
    n_gy = lax.axis_size("gy")
    blocks, markers = marker_cell.shape
    width = n_gx * SLOT * markers
    marker_rows = (3, blocks, markers)
    packed = (n_gx, 8, markers)
    f32, bf16, i32 = jnp.float32, jnp.bfloat16, jnp.int32
    dma = pltpu.SemaphoreType.DMA
    vmem = pltpu.VMEM
    in_hbm = functools.partial(pltpu.with_memory_space_constraint, memory_space=pltpu.HBM)
    in_vmem = functools.partial(pltpu.with_memory_space_constraint, memory_space=pltpu.VMEM)
    anywhere = pl.BlockSpec(memory_space=pl.ANY)
    inside = pl.BlockSpec(memory_space=pltpu.VMEM)
    state, force = pl.pallas_call(
        functools.partial(kernel, n_gx, n_gy),
        out_shape=(vmem(populations.shape, f32), vmem(marker_rows, f32)),
        in_specs=[anywhere] * 8,
        out_specs=(inside, inside),
        scratch_shapes=[
            vmem(populations.shape, f32),
            vmem(populations.shape, f32),
            vmem((5, CX, CY, NZ), f32),
            vmem(flags.shape, i32),
            pltpu.SMEM((1, blocks), i32),
            vmem(marker_cell.shape, i32),
            vmem(marker_rows, f32),
            vmem(marker_live.shape, i32),
            vmem(marker_rows, f32),
            vmem(marker_rows, f32),
            vmem(marker_rows, f32),
            vmem(marker_rows, f32),
        ]
        + [vmem(packed, f32)] * 10
        + [
            vmem((2 * NZ, width), bf16),
            vmem((width, 2 * NZ), bf16),
            vmem((COLS, width), f32),
            vmem((6 * COLS, width), bf16),
            vmem((6 * COLS, 2 * NZ), bf16),
            vmem(populations.shape, f32),
            vmem((2, 24, NZ), f32),
            vmem((2, 24, NZ), f32),
            vmem((8, CY, NZ), f32),
            vmem((8, CY, NZ), f32),
            vmem((STEPS, 2, 5, CY, NZ), f32),
            vmem((STEPS, 2, 5, CY, NZ), f32),
            vmem((STEPS, 2, 24, NZ), f32),
            vmem((STEPS, 2, 24, NZ), f32),
            vmem((STEPS, 4, 8, NZ), f32),
            vmem((STEPS, 4, 8, NZ), f32),
            dma((8,)),
        ]
        + [dma((n_gx,))] * 8
        + [dma((8,))] * 2
        + [dma((STEPS, 8))] * 2,
        compiler_params=pltpu.CompilerParams(
            collective_id=0,
            has_side_effects=True,
            vmem_limit_bytes=32 * 1024 * 1024,
        ),
    )(
        in_hbm(populations),
        in_hbm(flags),
        in_hbm(block_tile.T),
        in_hbm(marker_cell),
        in_hbm(marker_frac.transpose(1, 0, 2)),
        in_hbm(marker_live),
        in_hbm(marker_target.transpose(1, 0, 2)),
        in_hbm(marker_force.transpose(1, 0, 2)),
    )
    state, force = pl.pallas_call(
        deliver,
        out_shape=(
            jax.ShapeDtypeStruct(populations.shape, f32),
            jax.ShapeDtypeStruct(marker_rows, f32),
        ),
        in_specs=[inside] * 2,
        out_specs=(anywhere, anywhere),
        scratch_shapes=[dma((2,))],
    )(in_vmem(state), in_vmem(force))
    return state, force.transpose(1, 0, 2)


def solution(mesh):
    in_specs = (
        P(None, "gx", "gy", None),
        P("gx", "gy", None),
        P(("gx", "gy"), None),
        P(("gx", "gy"), None),
        P(("gx", "gy"), None, None),
        P(("gx", "gy"), None),
        P(("gx", "gy"), None, None),
        P(("gx", "gy"), None, None),
    )
    out_specs = (P(None, "gx", "gy", None), P(("gx", "gy"), None, None))
    return jax.shard_map(body, mesh=mesh, in_specs=in_specs, out_specs=out_specs, check_vma=False)
```
